512 devices in a mesh: scen: 8 (over x, core), dom: 64 (over z, y).
Axes of the slice: x: 4, y: 4, z: 16, core: 2. Of those that a mesh axis runs over, the one named last changes fastest.
Arguments:
- demand: int32 [2048, 2048], P('dom', 'scen'), may hold values from 0 to 17, as said below
- recourse_init: float32 [2048, 2048], P('dom', 'scen'), may hold values from 0 to 4
- transship: bfloat16 [2048, 2048], P('dom'), may hold values from -0.125 to 0.125
- counts: int32 [2048], P('scen'), may hold values from 1 to 8
- assign: int32 [65536], P('dom'), may hold values from 0 to 2047, as said below
- hold_cost: float32 [65536], P('dom'), may hold values from 0.2 to 3
- stock_init: float32 [65536], P('dom'), may hold values from 0 to 0.5
- mult_init: float32 [8, 65536], P('scen', 'dom'), may hold values from -3 to 3
Outputs:
- consensus: float32 [65536], P('dom')
- multipliers: float32 [8, 65536], P('scen', 'dom')
- recourse: float32 [2048, 2048], P('dom', 'scen')
The draws below stay inside these ranges and needn't reach their ends.
Inputs may be any that keep to these rules, and one draw needn't show every extreme that they name: Sites of higher index have no smaller range of demand. `assign`: parts of the p-th block of 1024 parts are stocked at sites of the p-th block of 32 sites.
All inputs are finite; a program needn't handle non-finite values.
Results may differ from the reference program's by a relative error of at most 0.0004.
Values may be sent and summed in bfloat16 or wider, within the bound.
No kernel may reach another device: no remote copies, remote signals or barrier semaphores. Data moves between devices by JAX's collectives and lax.ppermute only.
A program may use at most 64 MiB of HBM per device.

```python
import jax
import jax.numpy as jnp
from jax import lax

SITE_COUNT = 2048
PART_DEV = 1024
GROUP_SCENARIOS = 256
PARTS_SIZE = 65536
TOTAL_SCENARIOS = 2048
SCENARIO_GROUPS = 8


def draw_demand(key, part):
    key = jax.random.fold_in(key, 11)
    site = jnp.arange(SITE_COUNT, dtype=jnp.int32)[:, None]
    top = 7 + 12 * site // SITE_COUNT
    raw = jax.random.randint(key, (SITE_COUNT, TOTAL_SCENARIOS), 0, 1048576, dtype=jnp.int32)
    return raw % top


def draw_assign(key, part):
    key = jax.random.fold_in(key, 23)
    part_ids = jnp.arange(PARTS_SIZE, dtype=jnp.int32)
    site_block = SITE_COUNT * PART_DEV // PARTS_SIZE
    offset = jax.random.randint(key, (PARTS_SIZE,), 0, site_block, dtype=jnp.int32)
    return part_ids // PART_DEV * site_block + offset


def plant(entries, rng, least, high):
    index_at = [jax.random.randint(jax.random.fold_in(rng, axis), (), 0, length) for axis, length in enumerate(entries.shape)]
    main_axis = entries.shape.index(max(entries.shape))
    neighbour = index_at[:main_axis] + [(index_at[main_axis] + 1) % entries.shape[main_axis]] + index_at[main_axis + 1:]
    return entries.at[tuple(index_at)].set(least).at[tuple(neighbour)].set(high)


def block_levels(rng, dims, split, smallest, top_value):
    loudness = 1.0
    for axis_at, parts in split:
        steps = jax.random.uniform(jax.random.fold_in(jax.random.fold_in(rng, 6), axis_at), (parts,), jnp.float32, smallest / len(split), top_value / len(split))
        loudness = loudness * jnp.repeat(jnp.exp(steps), dims[axis_at] // parts).reshape((-1,) + (1,) * (len(dims) - 1 - axis_at))
    return loudness


def scatter_about(stream_key, dims, deviation, reach, pieces=(), kind=jnp.bfloat16):
    array = jax.random.normal(stream_key, dims, jnp.float32) * deviation
    if len(pieces) > 0:
        array = block_levels(stream_key, dims, pieces, -0.22, 0.18) * array
    return jnp.clip(array, min=-reach, max=reach).astype(kind)


def setup_inputs(seed: int = 0) -> dict:
    arg_keys = jax.random.split(jax.random.key(seed), 9)
    demand = draw_demand(jax.random.fold_in(arg_keys[8], 71), 0)
    recourse_init = jnp.clip(4.0 * jax.random.uniform(arg_keys[1], (SITE_COUNT, TOTAL_SCENARIOS), jnp.float32) ** block_levels(arg_keys[1], (SITE_COUNT, TOTAL_SCENARIOS), ((0, 64), (1, 8)), -0.2, 0.2), 0.0, 4.0)
    transship = scatter_about(arg_keys[2], (SITE_COUNT, SITE_COUNT), SITE_COUNT ** -0.5, 0.125, ((0, 64),))
    counts = plant(jax.random.randint(arg_keys[3], (TOTAL_SCENARIOS,), 1, 9), jax.random.fold_in(arg_keys[3], 1), 1, 8).astype(jnp.int32)
    assign = draw_assign(jax.random.fold_in(arg_keys[8], 71), 0)
    hold_cost = jnp.clip(0.2 + 2.8 * jax.random.uniform(arg_keys[5], (PARTS_SIZE,), jnp.float32) ** block_levels(arg_keys[5], (PARTS_SIZE,), ((0, 64),), -0.2, 0.2), 0.2, 3.0)
    stock_init = jnp.clip(0.5 * jax.random.uniform(arg_keys[6], (PARTS_SIZE,), jnp.float32) ** block_levels(arg_keys[6], (PARTS_SIZE,), ((0, 64),), -0.2, 0.2), 0.0, 0.5)
    mult_init = scatter_about(arg_keys[7], (SCENARIO_GROUPS, PARTS_SIZE), 0.5, 3.0, ((0, 8), (1, 64)), jnp.float32)
    return dict(demand=demand, recourse_init=recourse_init, transship=transship, counts=counts, assign=assign, hold_cost=hold_cost, stock_init=stock_init, mult_init=mult_init)


penalty = 1.0
stride = 0.5
prox_weight = 2.0
learn_rate = 0.05
epsilon = 1e-05

def reference(demand, recourse_init, transship, counts, assign, hold_cost, stock_init, mult_init):
    weights = counts.astype(jnp.float32).reshape(SCENARIO_GROUPS, GROUP_SCENARIOS)
    group_total = lax.optimization_barrier(jnp.sum(weights, axis=1))
    share = weights / group_total[:, None]
    stock = jnp.broadcast_to(stock_init[None, :], (SCENARIO_GROUPS, PARTS_SIZE))
    consensus = stock_init
    multipliers = mult_init
    recourse = recourse_init
    demand_draw = demand.astype(jnp.float32).reshape(SITE_COUNT, SCENARIO_GROUPS, GROUP_SCENARIOS)
    for outer in range(2):
        stock_by_site = jax.vmap(lambda row: jax.ops.segment_sum(row, assign, SITE_COUNT))(stock)
        shortfall = (demand_draw - stock_by_site.T[:, :, None]).reshape(SITE_COUNT, TOTAL_SCENARIOS)
        for inner in range(2):
            image = jnp.dot(transship, recourse.astype(jnp.bfloat16), preferred_element_type=jnp.float32)
            grad = image - penalty * (shortfall - recourse)
            scale = jnp.sqrt(lax.optimization_barrier(jnp.mean(grad * grad, axis=0)) + epsilon)
            recourse = jnp.maximum(recourse - stride * grad / scale[None, :], 0.0)
        gap = (shortfall - recourse).reshape(SITE_COUNT, SCENARIO_GROUPS, GROUP_SCENARIOS)
        pull = penalty * jnp.einsum('sgk,gk->gs', gap, share, precision=lax.Precision.HIGHEST)
        pull_parts = pull[:, assign]
        step = hold_cost[None, :] + multipliers - pull_parts + prox_weight * (stock - consensus[None, :])
        stock = jnp.maximum(stock - learn_rate * step, 0.0)
        consensus = lax.optimization_barrier(jnp.sum(group_total[:, None] * stock, axis=0)) / jnp.sum(group_total)
        multipliers = multipliers + prox_weight * (stock - consensus[None, :])
    return (consensus, multipliers, recourse)
```

```python
import functools

import jax
import jax.numpy as jnp
from jax import lax
from jax.experimental import pallas as pl
from jax.experimental.pallas import tpu as pltpu
from jax.sharding import Mesh, PartitionSpec as P

SITE_COUNT = 2048
X, CORE, Z, Y = 4, 2, 16, 4
ROWS = 32
COLS = 256
SCEN = 64
PACK = 56

penalty = 1.0
stride = 0.5
prox_weight = 2.0
learn_rate = 0.05
epsilon = 1e-05


def gather_blocks(block, axes, count):
    spread = jnp.broadcast_to(block[None], (count,) + block.shape)
    return lax.all_to_all(spread, axes, 0, 0, tiled=True)


def to_column(row, start):
    lane = lax.broadcasted_iota(jnp.int32, (ROWS, 128), 1)
    sub = lax.broadcasted_iota(jnp.int32, (ROWS, 128), 0)
    picked = jnp.where(lane == sub + start, jnp.broadcast_to(row, (ROWS, 128)), 0.0)
    return jnp.sum(picked, axis=1, keepdims=True)


def recourse_steps(core_ref, mine_ref, other_ref, rec_ref, short_ref, grad_ref, rounded_ref):
    core = core_ref[0]
    for inner in range(2):

        def tile(j, square):
            y = j // 2
            half = j % 2
            acc = jnp.zeros((256, 128), jnp.float32)
            for x in range(X):
                for ref, chunk in ((mine_ref, 2 * x + core), (other_ref, 2 * x + 1 - core)):
                    at = pl.multiple_of(chunk * COLS, COLS)
                    rows = pl.ds(pl.multiple_of(half * 256, 256), 256)
                    acc = acc + jnp.dot(
                        ref[x * Y + y, rows, :],
                        rounded_ref[pl.ds(at, COLS), :],
                        preferred_element_type=jnp.float32,
                    )
            for k in range(8):
                at = pl.ds(pl.multiple_of(((half * 8 + k) * Y + y) * ROWS, ROWS), ROWS)
                grad = acc[k * ROWS : (k + 1) * ROWS] - penalty * (short_ref[at, :] - rec_ref[at, :])
                grad_ref[at, :] = grad
                square = square + grad * grad
            return square

        square = lax.fori_loop(0, 8, tile, jnp.zeros((ROWS, 128), jnp.float32))
        square = jnp.sum(square, axis=0, keepdims=True)
        factor = stride / jnp.sqrt(square / SITE_COUNT + epsilon)

        def renew(j, carry):
            at = pl.ds(pl.multiple_of(j * 256, 256), 256)
            rec = jnp.maximum(rec_ref[at, :] - grad_ref[at, :] * factor, 0.0)
            rec_ref[at, :] = rec
            rounded_ref[at, :] = rec.astype(jnp.bfloat16)
            return carry

        lax.fori_loop(0, 8, renew, 0)


def pull_sums(share_ref, rec_ref, short_ref, pull_ref):
    for j in range(8):
        at = pl.ds(j * 256, 256)
        gap = short_ref[at, :] - rec_ref[at, :]
        pull_ref[:, at] = penalty * lax.dot_general(
            share_ref[...],
            gap,
            (((1,), (1,)), ((), ())),
            precision=lax.Precision.HIGHEST,
            preferred_element_type=jnp.float32,
        )


def first_kernel(
    core_ref, share_ref, mine_ref, other_ref, pack_ref, rec_ref, short_ref, pull_ref, grad_ref, rounded_ref
):
    def load(b, carry):
        at = pl.ds(pl.multiple_of(b * ROWS, ROWS), ROWS)
        both = pack_ref[b, 0:ROWS, :]
        rec_ref[at, :] = both
        rounded_ref[at, :] = both.astype(jnp.bfloat16)
        short_ref[at, :] = pltpu.roll(both, SCEN, 1)
        return carry

    lax.fori_loop(0, Z * Y, load, 0)
    recourse_steps(core_ref, mine_ref, other_ref, rec_ref, short_ref, grad_ref, rounded_ref)
    pull_sums(share_ref, rec_ref, short_ref, pull_ref)


def second_kernel(
    core_ref,
    share_ref,
    mine_ref,
    other_ref,
    pack_ref,
    rec_in_ref,
    short_in_ref,
    pulled_ref,
    rec_ref,
    pull_ref,
    short_ref,
    grad_ref,
    rounded_ref,
):
    def load(b, carry):
        at = pl.ds(pl.multiple_of(b * ROWS, ROWS), ROWS)
        z = b // Y
        y = b % Y
        pull = to_column(pulled_ref[pl.ds(z, 1), :], y * ROWS)
        site = lax.broadcasted_iota(jnp.int32, (ROWS, 128), 0).astype(jnp.float32)
        total = jnp.zeros((ROWS, 128), jnp.float32)
        gain = jnp.broadcast_to(learn_rate * pull, (ROWS, 128))
        for k in range(8):
            base = pack_ref[b, ROWS + k : ROWS + k + 1, :]
            index = pack_ref[b, ROWS + 8 + k : ROWS + 9 + k, :]
            stock = jnp.maximum(base + gain, 0.0)
            total = total + jnp.where(index == site, stock, 0.0)
        new_sum = jnp.sum(total, axis=1, keepdims=True)
        old_sum = to_column(pack_ref[b, ROWS + 16 : ROWS + 17, :], 0)
        rec = rec_in_ref[at, :]
        rec_ref[at, :] = rec
        rounded_ref[at, :] = rec.astype(jnp.bfloat16)
        short_ref[at, :] = short_in_ref[at, :] + (old_sum - new_sum)
        return carry

    lax.fori_loop(0, Z * Y, load, 0)
    recourse_steps(core_ref, mine_ref, other_ref, rec_ref, short_ref, grad_ref, rounded_ref)
    pull_sums(share_ref, rec_ref, short_ref, pull_ref)


def run_kernel(kernel, outs, scratch, *args):
    vmem = pl.BlockSpec(memory_space=pltpu.VMEM)
    return pl.pallas_call(
        kernel,
        out_shape=outs,
        in_specs=[pl.BlockSpec(memory_space=pltpu.SMEM)] + [vmem] * (len(args) - 1),
        out_specs=[vmem] * len(outs),
        scratch_shapes=scratch,
        compiler_params=pltpu.CompilerParams(vmem_limit_bytes=40 * 1024 * 1024),
    )(*args)


def per_device(demand, recourse_init, transship, counts, assign, hold_cost, stock_init, mult_init):
    core = lax.axis_index("core")
    column = lax.axis_index("x") * CORE + core
    y = lax.axis_index("y")
    z = lax.axis_index("z")
    f32 = jnp.float32
    wide = jax.ShapeDtypeStruct((SITE_COUNT, 128), f32)
    sums = jax.ShapeDtypeStruct((8, SITE_COUNT), f32)

    multipliers = mult_init[0]
    local_site = assign - (z * Y + y) * ROWS
    member = (local_site[:, None] == jnp.arange(ROWS, dtype=jnp.int32)[None, :]).astype(f32)
    stock_sum = jnp.dot(stock_init, member, precision=lax.Precision.HIGHEST)
    short = demand.astype(f32) - stock_sum[:, None]
    base = stock_init - learn_rate * (hold_cost + multipliers)
    sites = jnp.concatenate(
        [recourse_init.reshape(ROWS, Y, SCEN), short.reshape(ROWS, Y, SCEN)], axis=2
    ).transpose(1, 0, 2)
    parts = jnp.concatenate(
        [
            base.reshape(8, 128),
            local_site.astype(f32).reshape(8, 128),
            jnp.broadcast_to(jnp.pad(stock_sum, (0, 128 - ROWS))[None], (8, 128)),
        ],
        axis=0,
    )
    packed = jnp.concatenate([sites, jnp.broadcast_to(parts[None], (Y,) + parts.shape)], axis=1)
    packed = lax.all_to_all(packed, "y", 0, 0, tiled=True)
    packed = lax.all_gather(packed, "z", axis=0, tiled=True)

    block = lax.dynamic_slice(transship, (0, column * COLS), (ROWS, COLS))
    along_z = gather_blocks(block, "z", Z).reshape(Z * ROWS, COLS)
    mine = gather_blocks(along_z, ("x", "y"), X * Y)
    other = lax.ppermute(mine, "core", [(0, 1), (1, 0)])

    weights = counts.astype(f32)
    total = jnp.sum(weights)
    share = lax.dynamic_slice(weights / total, (y * SCEN,), (SCEN,))
    share = jnp.broadcast_to(jnp.pad(share, (0, 128 - SCEN))[None], (8, 128))
    core_arr = core.reshape(1).astype(jnp.int32)

    vm = pltpu.VMEM
    rec, short_all, pull1 = run_kernel(
        first_kernel,
        [wide, wide, sums],
        [vm((SITE_COUNT, 128), f32), vm((SITE_COUNT, 128), jnp.bfloat16)],
        core_arr,
        share,
        mine,
        other,
        packed,
    )
    pull1 = lax.psum(pull1[0].reshape(Z, Y * ROWS), "y")
    rec, pull2 = run_kernel(
        second_kernel,
        [wide, sums],
        [vm((SITE_COUNT, 128), f32), vm((SITE_COUNT, 128), f32), vm((SITE_COUNT, 128), jnp.bfloat16)],
        core_arr,
        share,
        mine,
        other,
        packed,
        rec,
        short_all,
        pull1,
    )
    own = lax.dynamic_slice(rec, (z * Y * ROWS, 0), (Y * ROWS, SCEN)).reshape(Y, ROWS, SCEN)
    own = lax.all_to_all(own, "y", 0, 0, tiled=True)
    recourse = own.transpose(1, 0, 2).reshape(ROWS, Y * SCEN)

    pull2 = pull2[0].reshape(Z, Y * ROWS)
    pulls = jnp.concatenate(
        [
            lax.dynamic_index_in_dim(pull1, z, 0, False).reshape(Y, 1, ROWS),
            lax.dynamic_index_in_dim(pull2, z, 0, False).reshape(Y, 1, ROWS),
            jnp.broadcast_to(total, (Y, 1, 64)),
        ],
        axis=2,
    )
    send = jnp.concatenate(
        [
            jnp.broadcast_to(multipliers.reshape(1, 8, 128), (Y, 8, 128)),
            jnp.broadcast_to(pulls, (Y, 8, 128)),
        ],
        axis=1,
    )
    send = jnp.broadcast_to(send[None], (X * CORE,) + send.shape).reshape(X * CORE * Y, 16, 128)
    got = lax.all_to_all(send, ("x", "core", "y"), 0, 0, tiled=True).reshape(X * CORE, Y, 16, 128)
    mult = lax.dynamic_index_in_dim(got, y, 1, False)[:, :8].reshape(X * CORE, 1024)
    group_total = got[:, 0, 8, 64][:, None]
    pull1 = got[:, 0, 8, 0:ROWS]
    pull2 = jnp.sum(got[:, :, 8, ROWS : 2 * ROWS], axis=1)
    pulls = jnp.dot(
        jnp.concatenate([pull1, pull2], axis=0), member.T, precision=lax.Precision.HIGHEST
    )
    step = hold_cost[None] + mult - pulls[: X * CORE]
    stock = jnp.maximum(stock_init[None] - learn_rate * step, 0.0)
    all_total = jnp.sum(group_total)
    consensus = jnp.sum(group_total * stock, axis=0) / all_total
    mult = mult + prox_weight * (stock - consensus[None])
    step = hold_cost[None] + mult - pulls[X * CORE :] + prox_weight * (stock - consensus[None])
    stock = jnp.maximum(stock - learn_rate * step, 0.0)
    consensus = jnp.sum(group_total * stock, axis=0) / all_total
    mult = mult + prox_weight * (stock - consensus[None])
    mult = lax.dynamic_slice(mult, (column, 0), (1, 1024))
    return (consensus, mult, recourse)


def solution(mesh):
    grid = Mesh(mesh.devices.reshape(X, CORE, Z, Y), ("x", "core", "z", "y"))
    scen, dom = ("x", "core"), ("z", "y")
    in_specs = (
        P(dom, scen),
        P(dom, scen),
        P(dom, None),
        P(scen),
        P(dom),
        P(dom),
        P(dom),
        P(scen, dom),
    )
    out_specs = (P(dom), P(scen, dom), P(dom, scen))
    return jax.shard_map(
        per_device, mesh=grid, in_specs=in_specs, out_specs=out_specs, check_vma=False
    )
```

```python
import jax
import jax.numpy as jnp
from jax import lax
from jax.experimental import pallas as pl
from jax.experimental.pallas import tpu as pltpu
from jax.sharding import Mesh, PartitionSpec as P

SITE_COUNT = 2048
X, CORE, Z, Y = 4, 2, 16, 4
GROUPS = X * CORE
ROWS = 32
COLS = 256
SCEN = 64
PARTS = 24

penalty = 1.0
stride = 0.5
prox_weight = 2.0
learn_rate = 0.05
epsilon = 1e-05

f32 = jnp.float32


def lanes_of(shape):
    return lax.broadcasted_iota(jnp.int32, shape, len(shape) - 1)


def rows_of(shape):
    return lax.broadcasted_iota(jnp.int32, shape, len(shape) - 2)


def pick(row, index):
    return jnp.take_along_axis(
        jnp.broadcast_to(row, (8, 128)), index, axis=1, mode="promise_in_bounds"
    )


def prep_kernel(
    place_ref, demand_ref, rec_ref, counts_ref, assign_ref, hold_ref, stock_ref, mult_ref, packed_ref, aux_ref
):
    z, y = place_ref[1], place_ref[2]
    weights = counts_ref[...].astype(f32)
    total = jnp.sum(jnp.sum(weights, axis=1, keepdims=True), axis=0, keepdims=True)
    row = jnp.where(y >= 2, weights[1:2], weights[0:1])
    row = jnp.where(y % 2 == 1, pltpu.roll(row, SCEN, 1), row) / total
    row = jnp.where(lanes_of((1, 128)) < SCEN, row, 0.0)
    aux_ref[0:8, :] = jnp.broadcast_to(row, (8, 128))
    aux_ref[8:16, :] = jnp.broadcast_to(total, (8, 128))

    index = assign_ref[...] - (z * Y + y) * ROWS
    stock = stock_ref[...]
    site = rows_of((ROWS, 128))
    sums = jnp.zeros((ROWS, 128), f32)
    for k in range(8):
        sums = sums + jnp.where(index[k : k + 1] == site, stock[k : k + 1], 0.0)
    column = jnp.sum(sums, axis=1, keepdims=True)
    as_row = jnp.sum(jnp.where(lanes_of((ROWS, 128)) == site, column, 0.0), axis=0, keepdims=True)
    base = stock - learn_rate * (hold_ref[...] + mult_ref[...])
    low = lanes_of((ROWS, 128)) < SCEN
    for q in range(Y):
        tile = slice(q // 2 * 128, q // 2 * 128 + 128)
        rec = rec_ref[:, tile]
        short = demand_ref[:, tile].astype(f32) - column
        if q % 2 == 0:
            both = jnp.where(low, rec, pltpu.roll(short, SCEN, 1))
        else:
            both = jnp.where(low, pltpu.roll(rec, SCEN, 1), short)
        packed_ref[q, 0:ROWS, :] = both
        packed_ref[q, ROWS : ROWS + 8, :] = base
        packed_ref[q, ROWS + 8 : ROWS + 16, :] = index.astype(f32)
        packed_ref[q, ROWS + 16 : ROWS + 24, :] = jnp.broadcast_to(as_row, (8, 128))


def spread_z_kernel(place_ref, transship_ref, packed_ref, spread_ref, parts_ref):
    parts_ref[...] = packed_ref[:, ROWS:, :]
    at = pl.ds(pl.multiple_of(place_ref[3] * COLS, COLS), COLS)
    block = transship_ref[:, at]
    for z in range(Z):
        spread_ref[z] = block


def recourse_steps(core, mine_ref, other_ref, rec_ref, short_ref, grad_ref, rounded_ref):
    def one_step(inner, carry):
        square = jnp.zeros((ROWS, 128), f32)
        for y in range(Y):
            acc = jnp.zeros((512, 128), f32)
            for x in range(X):
                for ref, chunk in ((mine_ref, 2 * x + core), (other_ref, 2 * x + 1 - core)):
                    at = pl.ds(pl.multiple_of(chunk * COLS, COLS), COLS)
                    acc = acc + jnp.dot(
                        ref[x * Y + y], rounded_ref[at, :], preferred_element_type=f32
                    )
            for z in range(Z):
                at = pl.ds((z * Y + y) * ROWS, ROWS)
                grad = acc[z * ROWS : (z + 1) * ROWS] - penalty * (short_ref[at, :] - rec_ref[at, :])
                grad_ref[at, :] = grad
                square = square + grad * grad
        square = jnp.sum(square, axis=0, keepdims=True)
        factor = stride / jnp.sqrt(square / SITE_COUNT + epsilon)
        for j in range(16):
            at = pl.ds(j * 128, 128)
            rec = jnp.maximum(rec_ref[at, :] - grad_ref[at, :] * factor, 0.0)
            rec_ref[at, :] = rec
            rounded_ref[at, :] = rec.astype(jnp.bfloat16)
        return carry

    lax.fori_loop(0, 2, one_step, 0)


def pull_sums(share, rec_ref, short_ref, put):
    for z in range(Z):
        at = pl.ds(z * 128, 128)
        gap = penalty * (short_ref[at, :] - rec_ref[at, :]) * share
        put(z, jnp.sum(gap.T, axis=0, keepdims=True))


def first_kernel(
    place_ref, aux_ref, mine_ref, other_ref, sites_ref, rec_ref, short_ref, pull_ref, grad_ref, rounded_ref
):
    def load(b, carry):
        at = pl.ds(pl.multiple_of(b * ROWS, ROWS), ROWS)
        both = sites_ref[b]
        rec_ref[at, :] = both
        rounded_ref[at, :] = both.astype(jnp.bfloat16)
        short_ref[at, :] = pltpu.roll(both, SCEN, 1)
        return carry

    lax.fori_loop(0, Z * Y, load, 0, unroll=8)
    recourse_steps(place_ref[0], mine_ref, other_ref, rec_ref, short_ref, grad_ref, rounded_ref)

    def put(z, row):
        for q in range(Y):
            pull_ref[q, z : z + 1, :] = row

    pull_sums(aux_ref[0:1, :], rec_ref, short_ref, put)


def second_kernel(
    place_ref,
    aux_ref,
    mine_ref,
    other_ref,
    parts_ref,
    rec_in_ref,
    short_in_ref,
    pulled_ref,
    mult_ref,
    send_ref,
    rec_ref,
    pull_ref,
    short_ref,
    grad_ref,
    rounded_ref,
):
    pull_ref[0] = pulled_ref[0] + pulled_ref[1] + pulled_ref[2] + pulled_ref[3]
    eye = lanes_of((ROWS, 128)) == rows_of((ROWS, 128))
    site = rows_of((ROWS, 128)).astype(f32)

    def load(b, carry):
        at = pl.ds(pl.multiple_of(b * ROWS, ROWS), ROWS)
        index = parts_ref[b, 8:16, :]
        pull = pick(pull_ref[0, pl.ds(b // Y, 1), :], index.astype(jnp.int32) + b % Y * ROWS)
        stock = jnp.maximum(parts_ref[b, 0:8, :] + learn_rate * pull, 0.0)
        change = jnp.where(eye, -parts_ref[b, 16:17, :], 0.0)
        for k in range(8):
            change = change + jnp.where(index[k : k + 1] == site, stock[k : k + 1], 0.0)
        rec = rec_in_ref[at, :]
        rec_ref[at, :] = rec
        rounded_ref[at, :] = rec.astype(jnp.bfloat16)
        short_ref[at, :] = short_in_ref[at, :] - jnp.sum(change, axis=1, keepdims=True)
        return carry

    lax.fori_loop(0, Z * Y, load, 0, unroll=8)
    recourse_steps(place_ref[0], mine_ref, other_ref, rec_ref, short_ref, grad_ref, rounded_ref)

    def put(z, row):
        pull_ref[1, z : z + 1, :] = row

    pull_sums(aux_ref[0:1, :], rec_ref, short_ref, put)
    z = place_ref[1]
    sub = rows_of((8, 128))
    pulls = jnp.where(
        sub == 0,
        pull_ref[0, pl.ds(z, 1), :],
        jnp.where(sub == 1, pull_ref[1, pl.ds(z, 1), :], aux_ref[8:9, :]),
    )
    low = lanes_of((16, 128)) < SCEN
    for q in range(Y):
        start = pl.multiple_of((z * Y + q) * ROWS, ROWS)
        upper = rec_ref[pl.ds(start, 16), :]
        lower = rec_ref[pl.ds(start + 16, 16), :]
        pair = jnp.where(low, upper, pltpu.roll(lower, SCEN, 1))
        for g in range(GROUPS):
            send_ref[g * Y + q, 0:8, :] = mult_ref[...]
            send_ref[g * Y + q, 8:16, :] = pulls
            send_ref[g * Y + q, 16:32, :] = pair


def last_kernel(
    place_ref, got_ref, assign_ref, hold_ref, stock_ref, consensus_ref, mult_ref, rec_ref, all_ref
):
    z, y, column = place_ref[1], place_ref[2], place_ref[3]
    index = assign_ref[...] - z * (Y * ROWS)
    hold = hold_ref[...]
    start = stock_ref[...]
    totals = [got_ref[g * Y, 10:11, :] for g in range(GROUPS)]
    all_total = totals[0]
    for g in range(1, GROUPS):
        all_total = all_total + totals[g]
    mults = [got_ref[g * Y + y, 0:8, :] for g in range(GROUPS)]
    stocks = []
    weighted = jnp.zeros((8, 128), f32)
    for g in range(GROUPS):
        pull = pick(got_ref[g * Y, 8:9, :], index)
        stock = jnp.maximum(start - learn_rate * (hold + mults[g] - pull), 0.0)
        weighted = weighted + totals[g] * stock
        stocks.append(stock)
    consensus = weighted / all_total
    weighted = jnp.zeros((8, 128), f32)
    for g in range(GROUPS):
        row = got_ref[g * Y, 9:10, :]
        for q in range(1, Y):
            row = row + got_ref[g * Y + q, 9:10, :]
        pull = pick(row, index)
        apart = prox_weight * (stocks[g] - consensus)
        mults[g] = mults[g] + apart
        stock = jnp.maximum(stocks[g] - learn_rate * (hold + mults[g] - pull + apart), 0.0)
        weighted = weighted + totals[g] * stock
        stocks[g] = stock
    consensus = weighted / all_total
    consensus_ref[...] = consensus
    for g in range(GROUPS):
        all_ref[g] = mults[g] + prox_weight * (stocks[g] - consensus)
    mult_ref[...] = all_ref[column]

    low = lanes_of((16, 128)) < SCEN
    for m in range(2):
        tile = slice(m * 128, m * 128 + 128)
        even = got_ref[column * Y + 2 * m, 16:32, :]
        odd = got_ref[column * Y + 2 * m + 1, 16:32, :]
        rec_ref[0:16, tile] = jnp.where(low, even, pltpu.roll(odd, SCEN, 1))
        rec_ref[16:32, tile] = jnp.where(low, pltpu.roll(even, SCEN, 1), odd)


def run_kernel(kernel, outs, scratch, *args):
    vmem = pl.BlockSpec(memory_space=pltpu.VMEM)
    outs = [out if isinstance(out, jax.ShapeDtypeStruct) else jax.ShapeDtypeStruct(out, f32) for out in outs]
    return pl.pallas_call(
        kernel,
        out_shape=outs,
        in_specs=[pl.BlockSpec(memory_space=pltpu.SMEM)] + [vmem] * (len(args) - 1),
        out_specs=[vmem] * len(outs),
        scratch_shapes=[pltpu.VMEM(*entry) for entry in scratch],
        compiler_params=pltpu.CompilerParams(vmem_limit_bytes=40 * 1024 * 1024),
    )(*args)


def one_block(always, work, *args):
    shapes = jax.eval_shape(work, *args)

    def never(*args):
        return jax.tree.map(lambda shape: jnp.zeros(shape.shape, shape.dtype), shapes)

    return lax.cond(always, work, never, *args)


def per_device(demand, recourse_init, transship, counts, assign, hold_cost, stock_init, mult_init):
    core = lax.axis_index("core")
    column = lax.axis_index("x") * CORE + core
    y = lax.axis_index("y")
    z = lax.axis_index("z")
    place = jnp.stack([core, z, y, column]).astype(jnp.int32)
    wide = (SITE_COUNT, 128)
    assign = assign.reshape(8, 128)
    hold_cost = hold_cost.reshape(8, 128)
    stock_init = stock_init.reshape(8, 128)
    mult_init = mult_init.reshape(8, 128)

    packed, aux = run_kernel(
        prep_kernel,
        [(Y, ROWS + PARTS, 128), (16, 128)],
        [],
        place,
        demand,
        recourse_init,
        counts.reshape(2, 128),
        assign,
        hold_cost,
        stock_init,
        mult_init,
    )
    packed = lax.all_to_all(packed, "y", 0, 0, tiled=True)
    sites = packed[:, :ROWS]

    bf16 = jnp.bfloat16
    always = column * COLS >= 0

    def spread_z(transship, packed):
        block, parts = run_kernel(
            spread_z_kernel,
            [jax.ShapeDtypeStruct((Z, ROWS, COLS), bf16), (Y, PARTS, 128)],
            [],
            place,
            transship,
            packed,
        )
        return lax.all_to_all(block, "z", 0, 0, tiled=True).reshape(Z * ROWS, COLS), parts

    def spread_xy(along_z):
        spread = jnp.broadcast_to(along_z[None], (X * Y, Z * ROWS, COLS))
        mine = lax.all_to_all(spread, ("x", "y"), 0, 0, tiled=True)
        return mine, lax.ppermute(mine, "core", [(0, 1), (1, 0)])

    sites = lax.all_gather(sites, "z", axis=0, tiled=True)
    along_z, parts = one_block(always, spread_z, transship, packed)
    parts = lax.all_gather(parts, "z", axis=0, tiled=True)
    mine, other = one_block(always, spread_xy, along_z)

    rec, short, pull1 = run_kernel(
        first_kernel,
        [wide, wide, (Y, Z, 128)],
        [(wide, f32), (wide, jnp.bfloat16)],
        place,
        aux,
        mine,
        other,
        sites,
    )
    pull1 = lax.all_to_all(pull1, "y", 0, 0, tiled=True)
    (send,) = run_kernel(
        second_kernel,
        [(GROUPS * Y, 32, 128)],
        [(wide, f32), ((2, Z, 128), f32), (wide, f32), (wide, f32), (wide, jnp.bfloat16)],
        place,
        aux,
        mine,
        other,
        parts,
        rec,
        short,
        pull1,
        mult_init,
    )
    got = lax.all_to_all(send, ("x", "core", "y"), 0, 0, tiled=True)
    consensus, multipliers, recourse = run_kernel(
        last_kernel,
        [(8, 128), (8, 128), (ROWS, Y * SCEN)],
        [((GROUPS, 8, 128), f32)],
        place,
        got,
        assign,
        hold_cost,
        stock_init,
    )
    return (consensus.reshape(1024), multipliers.reshape(1, 1024), recourse)


def solution(mesh):
    grid = Mesh(mesh.devices.reshape(X, CORE, Z, Y), ("x", "core", "z", "y"))
    scen, dom = ("x", "core"), ("z", "y")
    in_specs = (
        P(dom, scen),
        P(dom, scen),
        P(dom, None),
        P(scen),
        P(dom),
        P(dom),
        P(dom),
        P(scen, dom),
    )
    out_specs = (P(dom), P(scen, dom), P(dom, scen))
    return jax.shard_map(
        per_device, mesh=grid, in_specs=in_specs, out_specs=out_specs, check_vma=False
    )
```

```python
import jax
import jax.numpy as jnp
from jax import lax
from jax.experimental import pallas as pl
from jax.experimental.pallas import tpu as pltpu
from jax.sharding import Mesh, PartitionSpec as P

SITE_COUNT = 2048
X, CORE, Z, Y = 4, 2, 16, 4
GROUPS = X * CORE
ROWS = 32
COLS = 256
SCEN = 64
PARTS = 32

penalty = 1.0
stride = 0.5
prox_weight = 2.0
learn_rate = 0.05
epsilon = 1e-05

f32 = jnp.float32


def lanes_of(shape):
    return lax.broadcasted_iota(jnp.int32, shape, len(shape) - 1)


def rows_of(shape):
    return lax.broadcasted_iota(jnp.int32, shape, len(shape) - 2)


def pick(row, index):
    return jnp.take_along_axis(
        jnp.broadcast_to(row, (8, 128)), index, axis=1, mode="promise_in_bounds"
    )


def prep_kernel(place_ref, *refs):
    inputs, (packed_ref, aux_ref), copies = refs[:7], refs[7:9], refs[9:16]
    started = [
        pltpu.make_async_copy(source, target, refs[16].at[k])
        for k, (source, target) in enumerate(zip(inputs, copies))
    ]
    for copy in started:
        copy.start()
    for copy in started:
        copy.wait()
    demand_ref, rec_ref, counts_ref, assign_ref, hold_ref, stock_ref, mult_ref = copies
    z, y = place_ref[1], place_ref[2]
    weights = counts_ref[...].astype(f32)
    total = jnp.sum(jnp.sum(weights, axis=1, keepdims=True), axis=0, keepdims=True)
    row = jnp.where(y >= 2, weights[1:2], weights[0:1])
    row = jnp.where(y % 2 == 1, pltpu.roll(row, SCEN, 1), row) / total
    row = jnp.where(lanes_of((1, 128)) < SCEN, row, 0.0)
    aux_ref[0:8, :] = jnp.broadcast_to(row, (8, 128))
    aux_ref[8:16, :] = jnp.broadcast_to(total, (8, 128))

    index = assign_ref[...] - (z * Y + y) * ROWS
    stock = stock_ref[...]
    site = rows_of((ROWS, 128))
    sums = jnp.zeros((ROWS, 128), f32)
    for k in range(8):
        sums = sums + jnp.where(index[k : k + 1] == site, stock[k : k + 1], 0.0)
    column = jnp.sum(sums, axis=1, keepdims=True)
    as_row = jnp.sum(jnp.where(lanes_of((ROWS, 128)) == site, column, 0.0), axis=0, keepdims=True)
    base = stock - learn_rate * (hold_ref[...] + mult_ref[...])
    low = lanes_of((ROWS, 128)) < SCEN
    for q in range(Y):
        tile = slice(q // 2 * 128, q // 2 * 128 + 128)
        rec = rec_ref[:, tile]
        short = demand_ref[:, tile].astype(f32) - column
        if q % 2 == 0:
            both = jnp.where(low, rec, pltpu.roll(short, SCEN, 1))
        else:
            both = jnp.where(low, pltpu.roll(rec, SCEN, 1), short)
        packed_ref[q, 0:ROWS, :] = both
        packed_ref[q, ROWS : ROWS + 8, :] = base
        packed_ref[q, ROWS + 8 : ROWS + 16, :] = index.astype(f32)
        packed_ref[q, ROWS + 16 : ROWS + 32, :] = jnp.broadcast_to(as_row, (16, 128))


def spread_z_kernel(place_ref, transship_ref, packed_ref, spread_ref, parts_ref):
    parts_ref[...] = packed_ref[:, ROWS:, :]
    at = pl.ds(pl.multiple_of(place_ref[3] * COLS, COLS), COLS)
    block = transship_ref[:, at]
    for z in range(Z):
        spread_ref[z] = block


def recourse_steps(core, mine_ref, other_ref, rec_ref, short_ref, grad_ref, rounded_ref):
    def one_step(inner, carry):
        square = jnp.zeros((ROWS, 128), f32)
        for y in range(Y):
            acc = jnp.zeros((512, 128), f32)
            for x in range(X):
                for ref, chunk in ((mine_ref, 2 * x + core), (other_ref, 2 * x + 1 - core)):
                    at = pl.ds(pl.multiple_of(chunk * COLS, COLS), COLS)
                    acc = acc + jnp.dot(
                        ref[x * Y + y], rounded_ref[at, :], preferred_element_type=f32
                    )
            for z in range(Z):
                at = pl.ds((z * Y + y) * ROWS, ROWS)
                grad = acc[z * ROWS : (z + 1) * ROWS] - penalty * (short_ref[at, :] - rec_ref[at, :])
                grad_ref[at, :] = grad
                square = square + grad * grad
        square = jnp.sum(square, axis=0, keepdims=True)
        factor = stride / jnp.sqrt(square / SITE_COUNT + epsilon)

        def renew(j, carry):
            at = pl.ds(pl.multiple_of(j * 256, 256), 256)
            rec = jnp.maximum(rec_ref[at, :] - grad_ref[at, :] * factor, 0.0)
            rec_ref[at, :] = rec
            rounded_ref[at, :] = rec.astype(jnp.bfloat16)
            return carry

        lax.fori_loop(0, 8, renew, 0)
        return carry

    lax.fori_loop(0, 2, one_step, 0)


def pull_sums(share, rec_ref, short_ref, put):
    for z in range(Z):
        at = pl.ds(z * 128, 128)
        gap = penalty * (short_ref[at, :] - rec_ref[at, :]) * share
        put(z, jnp.sum(gap.T, axis=0, keepdims=True))


def first_kernel(
    place_ref, aux_ref, mine_ref, other_ref, sites_ref, rec_ref, short_ref, pull_ref, grad_ref, rounded_ref
):
    def load(b, carry):
        at = pl.ds(pl.multiple_of(b * ROWS, ROWS), ROWS)
        both = sites_ref[b]
        rec_ref[at, :] = both
        rounded_ref[at, :] = both.astype(jnp.bfloat16)
        short_ref[at, :] = pltpu.roll(both, SCEN, 1)
        return carry

    lax.fori_loop(0, Z * Y, load, 0, unroll=8)
    recourse_steps(place_ref[0], mine_ref, other_ref, rec_ref, short_ref, grad_ref, rounded_ref)

    def put(z, row):
        for q in range(Y):
            pull_ref[q, z : z + 1, :] = row

    pull_sums(aux_ref[0:1, :], rec_ref, short_ref, put)


def second_kernel(
    place_ref,
    aux_ref,
    mine_ref,
    other_ref,
    parts_ref,
    rec_in_ref,
    short_in_ref,
    pulled_ref,
    mult_ref,
    send_ref,
    rec_ref,
    pull_ref,
    short_ref,
    grad_ref,
    rounded_ref,
):
    pull_ref[0] = pulled_ref[0] + pulled_ref[1] + pulled_ref[2] + pulled_ref[3]
    eye = lanes_of((ROWS, 128)) == rows_of((ROWS, 128))
    site = rows_of((ROWS, 128)).astype(f32)

    def load(b, carry):
        at = pl.ds(pl.multiple_of(b * ROWS, ROWS), ROWS)
        index = parts_ref[b, 8:16, :]
        pull = pick(pull_ref[0, pl.ds(b // Y, 1), :], index.astype(jnp.int32) + b % Y * ROWS)
        stock = jnp.maximum(parts_ref[b, 0:8, :] + learn_rate * pull, 0.0)
        change = jnp.where(eye, -parts_ref[b, 16:17, :], 0.0)
        for k in range(8):
            change = change + jnp.where(index[k : k + 1] == site, stock[k : k + 1], 0.0)
        rec = rec_in_ref[at, :]
        rec_ref[at, :] = rec
        rounded_ref[at, :] = rec.astype(jnp.bfloat16)
        short_ref[at, :] = short_in_ref[at, :] - jnp.sum(change, axis=1, keepdims=True)
        return carry

    lax.fori_loop(0, Z * Y, load, 0, unroll=8)
    recourse_steps(place_ref[0], mine_ref, other_ref, rec_ref, short_ref, grad_ref, rounded_ref)

    def put(z, row):
        pull_ref[1, z : z + 1, :] = row

    pull_sums(aux_ref[0:1, :], rec_ref, short_ref, put)
    z = place_ref[1]
    sub = rows_of((8, 128))
    pulls = jnp.where(
        sub == 0,
        pull_ref[0, pl.ds(z, 1), :],
        jnp.where(sub == 1, pull_ref[1, pl.ds(z, 1), :], aux_ref[8:9, :]),
    )
    low = lanes_of((16, 128)) < SCEN
    for q in range(Y):
        start = pl.multiple_of((z * Y + q) * ROWS, ROWS)
        upper = rec_ref[pl.ds(start, 16), :]
        lower = rec_ref[pl.ds(start + 16, 16), :]
        pair = jnp.where(low, upper, pltpu.roll(lower, SCEN, 1))
        for g in range(GROUPS):
            send_ref[g * Y + q, 0:8, :] = mult_ref[...]
            send_ref[g * Y + q, 8:16, :] = pulls
            send_ref[g * Y + q, 16:32, :] = pair


def last_kernel(
    place_ref, got_ref, assign_ref, hold_ref, stock_ref, consensus_ref, mult_ref, rec_ref, all_ref
):
    z, y, column = place_ref[1], place_ref[2], place_ref[3]
    index = assign_ref[...] - z * (Y * ROWS)
    hold = hold_ref[...]
    start = stock_ref[...]
    totals = [got_ref[g * Y, 10:11, :] for g in range(GROUPS)]
    all_total = totals[0]
    for g in range(1, GROUPS):
        all_total = all_total + totals[g]
    mults = [got_ref[g * Y + y, 0:8, :] for g in range(GROUPS)]
    stocks = []
    weighted = jnp.zeros((8, 128), f32)
    for g in range(GROUPS):
        pull = pick(got_ref[g * Y, 8:9, :], index)
        stock = jnp.maximum(start - learn_rate * (hold + mults[g] - pull), 0.0)
        weighted = weighted + totals[g] * stock
        stocks.append(stock)
    consensus = weighted / all_total
    weighted = jnp.zeros((8, 128), f32)
    for g in range(GROUPS):
        row = got_ref[g * Y, 9:10, :]
        for q in range(1, Y):
            row = row + got_ref[g * Y + q, 9:10, :]
        pull = pick(row, index)
        apart = prox_weight * (stocks[g] - consensus)
        mults[g] = mults[g] + apart
        stock = jnp.maximum(stocks[g] - learn_rate * (hold + mults[g] - pull + apart), 0.0)
        weighted = weighted + totals[g] * stock
        stocks[g] = stock
    consensus = weighted / all_total
    consensus_ref[...] = consensus
    for g in range(GROUPS):
        all_ref[g] = mults[g] + prox_weight * (stocks[g] - consensus)
    mult_ref[...] = all_ref[column]

    low = lanes_of((16, 128)) < SCEN
    for m in range(2):
        tile = slice(m * 128, m * 128 + 128)
        even = got_ref[column * Y + 2 * m, 16:32, :]
        odd = got_ref[column * Y + 2 * m + 1, 16:32, :]
        rec_ref[0:16, tile] = jnp.where(low, even, pltpu.roll(odd, SCEN, 1))
        rec_ref[16:32, tile] = jnp.where(low, pltpu.roll(even, SCEN, 1), odd)


def run_kernel(kernel, outs, scratch, *args, hbm=0, vmem_mib=16):
    vmem = pl.BlockSpec(memory_space=pltpu.VMEM)
    outs = [out if isinstance(out, jax.ShapeDtypeStruct) else jax.ShapeDtypeStruct(out, f32) for out in outs]
    return pl.pallas_call(
        kernel,
        out_shape=outs,
        in_specs=[pl.BlockSpec(memory_space=pltpu.SMEM)]
        + [pl.BlockSpec(memory_space=pl.ANY)] * hbm
        + [vmem] * (len(args) - 1 - hbm),
        out_specs=[vmem] * len(outs),
        scratch_shapes=[pltpu.VMEM(*entry) if isinstance(entry, tuple) else entry for entry in scratch],
        compiler_params=pltpu.CompilerParams(vmem_limit_bytes=vmem_mib * 1024 * 1024),
    )(*args)


def one_block(always, work, *args):
    shapes = jax.eval_shape(work, *args)

    def never(*args):
        return jax.tree.map(lambda shape: jnp.zeros(shape.shape, shape.dtype), shapes)

    return lax.cond(always, work, never, *args)


def per_device(demand, recourse_init, transship, counts, assign, hold_cost, stock_init, mult_init):
    core = lax.axis_index("core")
    column = lax.axis_index("x") * CORE + core
    y = lax.axis_index("y")
    z = lax.axis_index("z")
    place = jnp.stack([core, z, y, column]).astype(jnp.int32)
    wide = (SITE_COUNT, 128)
    assign = assign.reshape(8, 128)
    hold_cost = hold_cost.reshape(8, 128)
    stock_init = stock_init.reshape(8, 128)
    mult_init = mult_init.reshape(8, 128)

    raw = (
        demand,
        recourse_init,
        counts.reshape(2, 128),
        assign,
        hold_cost,
        stock_init,
        mult_init,
    )
    packed, aux = run_kernel(
        prep_kernel,
        [(Y, ROWS + PARTS, 128), (16, 128)],
        [(entry.shape, entry.dtype) for entry in raw] + [pltpu.SemaphoreType.DMA((7,))],
        place,
        *raw,
        hbm=len(raw),
    )
    packed = lax.all_to_all(packed, "y", 0, 0, tiled=True)
    sites = packed[:, :ROWS]

    bf16 = jnp.bfloat16
    always = column * COLS >= 0

    def spread_z(transship, packed):
        block, parts = run_kernel(
            spread_z_kernel,
            [jax.ShapeDtypeStruct((Z, ROWS, COLS), bf16), (Y, PARTS, 128)],
            [],
            place,
            transship,
            packed,
        )
        return lax.all_to_all(block, "z", 0, 0, tiled=True).reshape(Z * ROWS, COLS), parts

    def spread_xy(along_z):
        spread = jnp.broadcast_to(along_z[None], (X * Y, Z * ROWS, COLS))
        return lax.all_to_all(spread, ("x", "y"), 0, 0, tiled=True)

    def swap_cores(mine):
        return lax.ppermute(mine, "core", [(0, 1), (1, 0)])

    sites = lax.all_gather(sites, "z", axis=0, tiled=True)
    along_z, parts = one_block(always, spread_z, transship, packed)
    parts = lax.all_gather(parts, "z", axis=0, tiled=True)
    mine = one_block(always, spread_xy, along_z)
    other = one_block(always, swap_cores, mine)

    rec, short, pull1 = run_kernel(
        first_kernel,
        [wide, wide, (Y, Z, 128)],
        [(wide, f32), (wide, jnp.bfloat16)],
        place,
        aux,
        mine,
        other,
        sites,
    )
    pull1 = lax.all_to_all(pull1, "y", 0, 0, tiled=True)
    (send,) = run_kernel(
        second_kernel,
        [(GROUPS * Y, 32, 128)],
        [(wide, f32), ((2, Z, 128), f32), (wide, f32), (wide, f32), (wide, jnp.bfloat16)],
        place,
        aux,
        mine,
        other,
        parts,
        rec,
        short,
        pull1,
        mult_init,
    )
    got = lax.all_to_all(send, ("x", "core", "y"), 0, 0, tiled=True)
    consensus, multipliers, recourse = run_kernel(
        last_kernel,
        [(8, 128), (8, 128), (ROWS, Y * SCEN)],
        [((GROUPS, 8, 128), f32)],
        place,
        got,
        assign,
        hold_cost,
        stock_init,
    )
    return (consensus.reshape(1024), multipliers.reshape(1, 1024), recourse)


def solution(mesh):
    grid = Mesh(mesh.devices.reshape(X, CORE, Z, Y), ("x", "core", "z", "y"))
    scen, dom = ("x", "core"), ("z", "y")
    in_specs = (
        P(dom, scen),
        P(dom, scen),
        P(dom, None),
        P(scen),
        P(dom),
        P(dom),
        P(dom),
        P(scen, dom),
    )
    out_specs = (P(dom), P(scen, dom), P(dom, scen))
    return jax.shard_map(
        per_device, mesh=grid, in_specs=in_specs, out_specs=out_specs, check_vma=False
    )
```

```python
import jax
import jax.numpy as jnp
from jax import lax
from jax.experimental import pallas as pl
from jax.experimental.pallas import tpu as pltpu
from jax.sharding import Mesh, PartitionSpec as P

SITE_COUNT = 2048
X, CORE, Z, Y = 4, 2, 16, 4
GROUPS = X * CORE
ROWS = 32
COLS = 256
SCEN = 64
PARTS = 24

penalty = 1.0
stride = 0.5
prox_weight = 2.0
learn_rate = 0.05
epsilon = 1e-05

f32 = jnp.float32


def lanes_of(shape):
    return lax.broadcasted_iota(jnp.int32, shape, len(shape) - 1)


def rows_of(shape):
    return lax.broadcasted_iota(jnp.int32, shape, len(shape) - 2)


def pick(row, index):
    return jnp.take_along_axis(
        jnp.broadcast_to(row, (8, 128)), index, axis=1, mode="promise_in_bounds"
    )


def prep_kernel(place_ref, *refs):
    inputs, (packed_ref, aux_ref), copies = refs[:7], refs[7:9], refs[9:16]
    started = [
        pltpu.make_async_copy(source, target, refs[16].at[k])
        for k, (source, target) in enumerate(zip(inputs, copies))
    ]
    for copy in started:
        copy.start()
    for copy in started:
        copy.wait()
    demand_ref, rec_ref, counts_ref, assign_ref, hold_ref, stock_ref, mult_ref = copies
    z, y = place_ref[1], place_ref[2]
    weights = counts_ref[...].astype(f32)
    total = jnp.sum(jnp.sum(weights, axis=1, keepdims=True), axis=0, keepdims=True)
    row = jnp.where(y >= 2, weights[1:2], weights[0:1])
    row = jnp.where(y % 2 == 1, pltpu.roll(row, SCEN, 1), row) / total
    row = jnp.where(lanes_of((1, 128)) < SCEN, row, 0.0)
    aux_ref[0:8, :] = jnp.broadcast_to(row, (8, 128))
    aux_ref[8:16, :] = jnp.broadcast_to(total, (8, 128))

    index = assign_ref[...] - (z * Y + y) * ROWS
    stock = stock_ref[...]
    site = rows_of((ROWS, 128))
    sums = jnp.zeros((ROWS, 128), f32)
    for k in range(8):
        sums = sums + jnp.where(index[k : k + 1] == site, stock[k : k + 1], 0.0)
    column = jnp.sum(sums, axis=1, keepdims=True)
    as_row = jnp.sum(jnp.where(lanes_of((ROWS, 128)) == site, column, 0.0), axis=0, keepdims=True)
    base = stock - learn_rate * (hold_ref[...] + mult_ref[...])
    low = lanes_of((ROWS, 128)) < SCEN
    for q in range(Y):
        tile = slice(q // 2 * 128, q // 2 * 128 + 128)
        rec = rec_ref[:, tile]
        short = demand_ref[:, tile].astype(f32) - column
        if q % 2 == 0:
            both = jnp.where(low, rec, pltpu.roll(short, SCEN, 1))
        else:
            both = jnp.where(low, pltpu.roll(rec, SCEN, 1), short)
        packed_ref[q, 0:ROWS, :] = both
        packed_ref[q, ROWS : ROWS + 8, :] = base
        packed_ref[q, ROWS + 8 : ROWS + 16, :] = index.astype(f32)
        packed_ref[q, ROWS + 16 : ROWS + 24, :] = jnp.broadcast_to(as_row, (8, 128))


def spread_z_kernel(place_ref, packed_ref, transship_ref, spread_ref):
    at = pl.ds(pl.multiple_of(place_ref[3] * COLS, COLS), COLS)
    block = transship_ref[:, at]
    for z in range(Z):
        spread_ref[z] = block


def recourse_steps(core, mine_ref, other_ref, rec_ref, short_ref, grad_ref, rounded_ref):
    def one_step(inner, carry):
        square = jnp.zeros((ROWS, 128), f32)
        for y in range(Y):
            acc = jnp.zeros((512, 128), f32)
            for x in range(X):
                for ref, chunk in ((mine_ref, 2 * x + core), (other_ref, 2 * x + 1 - core)):
                    at = pl.ds(pl.multiple_of(chunk * COLS, COLS), COLS)
                    acc = acc + jnp.dot(
                        ref[x * Y + y], rounded_ref[at, :], preferred_element_type=f32
                    )
            for z in range(Z):
                at = pl.ds((z * Y + y) * ROWS, ROWS)
                grad = acc[z * ROWS : (z + 1) * ROWS] - penalty * (short_ref[at, :] - rec_ref[at, :])
                grad_ref[at, :] = grad
                square = square + grad * grad
        square = jnp.sum(square, axis=0, keepdims=True)
        factor = stride / jnp.sqrt(square / SITE_COUNT + epsilon)

        def renew(j, carry):
            at = pl.ds(pl.multiple_of(j * 256, 256), 256)
            rec = jnp.maximum(rec_ref[at, :] - grad_ref[at, :] * factor, 0.0)
            rec_ref[at, :] = rec
            rounded_ref[at, :] = rec.astype(jnp.bfloat16)
            return carry

        lax.fori_loop(0, 8, renew, 0)
        return carry

    lax.fori_loop(0, 2, one_step, 0)


def pull_sums(share, rec_ref, short_ref, put):
    for z in range(Z):
        at = pl.ds(z * 128, 128)
        gap = penalty * (short_ref[at, :] - rec_ref[at, :]) * share
        put(z, jnp.sum(gap.T, axis=0, keepdims=True))


def first_kernel(
    place_ref, aux_ref, mine_ref, other_ref, packed_ref, rec_ref, short_ref, pull_ref, grad_ref, rounded_ref
):
    def load(b, carry):
        at = pl.ds(pl.multiple_of(b * ROWS, ROWS), ROWS)
        both = packed_ref[b, 0:ROWS, :]
        rec_ref[at, :] = both
        rounded_ref[at, :] = both.astype(jnp.bfloat16)
        short_ref[at, :] = pltpu.roll(both, SCEN, 1)
        return carry

    lax.fori_loop(0, Z * Y, load, 0, unroll=8)
    recourse_steps(place_ref[0], mine_ref, other_ref, rec_ref, short_ref, grad_ref, rounded_ref)

    def put(z, row):
        for q in range(Y):
            pull_ref[q, z : z + 1, :] = row

    pull_sums(aux_ref[0:1, :], rec_ref, short_ref, put)


def second_kernel(
    place_ref,
    aux_ref,
    mine_ref,
    other_ref,
    packed_ref,
    rec_in_ref,
    short_in_ref,
    pulled_ref,
    mult_ref,
    send_ref,
    rec_ref,
    pull_ref,
    short_ref,
    grad_ref,
    rounded_ref,
):
    pull_ref[0] = pulled_ref[0] + pulled_ref[1] + pulled_ref[2] + pulled_ref[3]
    eye = lanes_of((ROWS, 128)) == rows_of((ROWS, 128))
    site = rows_of((ROWS, 128)).astype(f32)

    def load(b, carry):
        at = pl.ds(pl.multiple_of(b * ROWS, ROWS), ROWS)
        index = packed_ref[b, ROWS + 8 : ROWS + 16, :]
        pull = pick(pull_ref[0, pl.ds(b // Y, 1), :], index.astype(jnp.int32) + b % Y * ROWS)
        stock = jnp.maximum(packed_ref[b, ROWS : ROWS + 8, :] + learn_rate * pull, 0.0)
        change = jnp.where(eye, -packed_ref[b, ROWS + 16 : ROWS + 17, :], 0.0)
        for k in range(8):
            change = change + jnp.where(index[k : k + 1] == site, stock[k : k + 1], 0.0)
        rec = rec_in_ref[at, :]
        rec_ref[at, :] = rec
        rounded_ref[at, :] = rec.astype(jnp.bfloat16)
        short_ref[at, :] = short_in_ref[at, :] - jnp.sum(change, axis=1, keepdims=True)
        return carry

    lax.fori_loop(0, Z * Y, load, 0, unroll=8)
    recourse_steps(place_ref[0], mine_ref, other_ref, rec_ref, short_ref, grad_ref, rounded_ref)

    def put(z, row):
        pull_ref[1, z : z + 1, :] = row

    pull_sums(aux_ref[0:1, :], rec_ref, short_ref, put)
    z = place_ref[1]
    sub = rows_of((8, 128))
    pulls = jnp.where(
        sub == 0,
        pull_ref[0, pl.ds(z, 1), :],
        jnp.where(sub == 1, pull_ref[1, pl.ds(z, 1), :], aux_ref[8:9, :]),
    )
    low = lanes_of((16, 128)) < SCEN
    for q in range(Y):
        start = pl.multiple_of((z * Y + q) * ROWS, ROWS)
        upper = rec_ref[pl.ds(start, 16), :]
        lower = rec_ref[pl.ds(start + 16, 16), :]
        pair = jnp.where(low, upper, pltpu.roll(lower, SCEN, 1))
        for g in range(GROUPS):
            send_ref[g * Y + q, 0:8, :] = mult_ref[...]
            send_ref[g * Y + q, 8:16, :] = pulls
            send_ref[g * Y + q, 16:32, :] = pair


def last_kernel(
    place_ref, got_ref, assign_ref, hold_ref, stock_ref, consensus_ref, mult_ref, rec_ref, all_ref
):
    z, y, column = place_ref[1], place_ref[2], place_ref[3]
    index = assign_ref[...] - z * (Y * ROWS)
    hold = hold_ref[...]
    start = stock_ref[...]
    totals = [got_ref[g * Y, 10:11, :] for g in range(GROUPS)]
    all_total = totals[0]
    for g in range(1, GROUPS):
        all_total = all_total + totals[g]
    mults = [got_ref[g * Y + y, 0:8, :] for g in range(GROUPS)]
    stocks = []
    weighted = jnp.zeros((8, 128), f32)
    for g in range(GROUPS):
        pull = pick(got_ref[g * Y, 8:9, :], index)
        stock = jnp.maximum(start - learn_rate * (hold + mults[g] - pull), 0.0)
        weighted = weighted + totals[g] * stock
        stocks.append(stock)
    consensus = weighted / all_total
    weighted = jnp.zeros((8, 128), f32)
    for g in range(GROUPS):
        row = got_ref[g * Y, 9:10, :]
        for q in range(1, Y):
            row = row + got_ref[g * Y + q, 9:10, :]
        pull = pick(row, index)
        apart = prox_weight * (stocks[g] - consensus)
        mults[g] = mults[g] + apart
        stock = jnp.maximum(stocks[g] - learn_rate * (hold + mults[g] - pull + apart), 0.0)
        weighted = weighted + totals[g] * stock
        stocks[g] = stock
    consensus = weighted / all_total
    consensus_ref[...] = consensus
    for g in range(GROUPS):
        all_ref[g] = mults[g] + prox_weight * (stocks[g] - consensus)
    mult_ref[...] = all_ref[column]

    low = lanes_of((16, 128)) < SCEN
    for m in range(2):
        tile = slice(m * 128, m * 128 + 128)
        even = got_ref[column * Y + 2 * m, 16:32, :]
        odd = got_ref[column * Y + 2 * m + 1, 16:32, :]
        rec_ref[0:16, tile] = jnp.where(low, even, pltpu.roll(odd, SCEN, 1))
        rec_ref[16:32, tile] = jnp.where(low, pltpu.roll(even, SCEN, 1), odd)


def run_kernel(kernel, outs, scratch, *args, hbm=0, vmem_mib=16):
    vmem = pl.BlockSpec(memory_space=pltpu.VMEM)
    outs = [out if isinstance(out, jax.ShapeDtypeStruct) else jax.ShapeDtypeStruct(out, f32) for out in outs]
    return pl.pallas_call(
        kernel,
        out_shape=outs,
        in_specs=[pl.BlockSpec(memory_space=pltpu.SMEM)]
        + [pl.BlockSpec(memory_space=pl.ANY)] * hbm
        + [vmem] * (len(args) - 1 - hbm),
        out_specs=[vmem] * len(outs),
        scratch_shapes=[pltpu.VMEM(*entry) if isinstance(entry, tuple) else entry for entry in scratch],
        compiler_params=pltpu.CompilerParams(vmem_limit_bytes=vmem_mib * 1024 * 1024),
    )(*args)


def one_block(always, work, *args):
    shapes = jax.eval_shape(work, *args)

    def never(*args):
        return jax.tree.map(lambda shape: jnp.zeros(shape.shape, shape.dtype), shapes)

    return lax.cond(always, work, never, *args)


def per_device(demand, recourse_init, transship, counts, assign, hold_cost, stock_init, mult_init):
    core = lax.axis_index("core")
    column = lax.axis_index("x") * CORE + core
    y = lax.axis_index("y")
    z = lax.axis_index("z")
    place = jnp.stack([core, z, y, column]).astype(jnp.int32)
    wide = (SITE_COUNT, 128)
    assign = assign.reshape(8, 128)
    hold_cost = hold_cost.reshape(8, 128)
    stock_init = stock_init.reshape(8, 128)
    mult_init = mult_init.reshape(8, 128)

    raw = (
        demand,
        recourse_init,
        counts.reshape(2, 128),
        assign,
        hold_cost,
        stock_init,
        mult_init,
    )
    packed, aux = run_kernel(
        prep_kernel,
        [(Y, ROWS + PARTS, 128), (16, 128)],
        [(entry.shape, entry.dtype) for entry in raw] + [pltpu.SemaphoreType.DMA((7,))],
        place,
        *raw,
        hbm=len(raw),
        vmem_mib=60,
    )
    packed = lax.all_to_all(packed, "y", 0, 0, tiled=True)
    bf16 = jnp.bfloat16
    always = column * COLS >= 0

    def spread_z(transship, packed):
        (block,) = run_kernel(
            spread_z_kernel,
            [jax.ShapeDtypeStruct((Z, ROWS, COLS), bf16)],
            [],
            place,
            packed,
            transship,
            hbm=1,
        )
        return lax.all_to_all(block, "z", 0, 0, tiled=True).reshape(Z * ROWS, COLS)

    def spread_xy(along_z):
        spread = jnp.broadcast_to(along_z[None], (X * Y, Z * ROWS, COLS))
        return lax.all_to_all(spread, ("x", "y"), 0, 0, tiled=True)

    def swap_cores(mine):
        return lax.ppermute(mine, "core", [(0, 1), (1, 0)])

    gathered = lax.all_gather(packed, "z", axis=0, tiled=True)
    along_z = one_block(always, spread_z, transship, packed)
    mine = one_block(always, spread_xy, along_z)
    other = one_block(always, swap_cores, mine)

    rec, short, pull1 = run_kernel(
        first_kernel,
        [wide, wide, (Y, Z, 128)],
        [(wide, f32), (wide, jnp.bfloat16)],
        place,
        aux,
        mine,
        other,
        gathered,
    )
    pull1 = lax.all_to_all(pull1, "y", 0, 0, tiled=True)
    (send,) = run_kernel(
        second_kernel,
        [(GROUPS * Y, 32, 128)],
        [(wide, f32), ((2, Z, 128), f32), (wide, f32), (wide, f32), (wide, jnp.bfloat16)],
        place,
        aux,
        mine,
        other,
        gathered,
        rec,
        short,
        pull1,
        mult_init,
    )
    got = lax.all_to_all(send, ("x", "core", "y"), 0, 0, tiled=True)
    consensus, multipliers, recourse = run_kernel(
        last_kernel,
        [(8, 128), (8, 128), (ROWS, Y * SCEN)],
        [((GROUPS, 8, 128), f32)],
        place,
        got,
        assign,
        hold_cost,
        stock_init,
    )
    return (consensus.reshape(1024), multipliers.reshape(1, 1024), recourse)


def solution(mesh):
    grid = Mesh(mesh.devices.reshape(X, CORE, Z, Y), ("x", "core", "z", "y"))
    scen, dom = ("x", "core"), ("z", "y")
    in_specs = (
        P(dom, scen),
        P(dom, scen),
        P(dom, None),
        P(scen),
        P(dom),
        P(dom),
        P(dom),
        P(scen, dom),
    )
    out_specs = (P(dom), P(scen, dom), P(dom, scen))
    return jax.shard_map(
        per_device, mesh=grid, in_specs=in_specs, out_specs=out_specs, check_vma=False
    )
```

```python
import jax
import jax.numpy as jnp
from jax import lax
from jax.experimental import pallas as pl
from jax.experimental.pallas import tpu as pltpu
from jax.sharding import Mesh, PartitionSpec as P

SITE_COUNT = 2048
X, CORE, Z, Y = 4, 2, 16, 4
GROUPS = X * CORE
ROWS = 32
COLS = 256
SCEN = 64
PARTS = 24
MIDDLE = Z + Z * 16 + Z

penalty = 1.0
stride = 0.5
prox_weight = 2.0
learn_rate = 0.05
epsilon = 1e-05

f32 = jnp.float32


def lanes_of(shape):
    return lax.broadcasted_iota(jnp.int32, shape, len(shape) - 1)


def rows_of(shape):
    return lax.broadcasted_iota(jnp.int32, shape, len(shape) - 2)


def pick(row, index):
    return jnp.take_along_axis(
        jnp.broadcast_to(row, (8, 128)), index, axis=1, mode="promise_in_bounds"
    )


def prep_kernel(place_ref, *refs):
    inputs, (packed_ref, aux_ref), copies = refs[:7], refs[7:9], refs[9:16]
    started = [
        pltpu.make_async_copy(source, target, refs[16].at[k])
        for k, (source, target) in enumerate(zip(inputs, copies))
    ]
    for copy in started:
        copy.start()
    for copy in started:
        copy.wait()
    demand_ref, rec_ref, counts_ref, assign_ref, hold_ref, stock_ref, mult_ref = copies
    z, y = place_ref[1], place_ref[2]
    weights = counts_ref[...].astype(f32)
    total = jnp.sum(jnp.sum(weights, axis=1, keepdims=True), axis=0, keepdims=True)
    row = jnp.where(y >= 2, weights[1:2], weights[0:1])
    row = jnp.where(y % 2 == 1, pltpu.roll(row, SCEN, 1), row) / total
    row = jnp.where(lanes_of((1, 128)) < SCEN, row, 0.0)
    aux_ref[0:8, :] = jnp.broadcast_to(row, (8, 128))
    aux_ref[8:16, :] = jnp.broadcast_to(total, (8, 128))

    index = assign_ref[...] - (z * Y + y) * ROWS
    stock = stock_ref[...]
    site = rows_of((ROWS, 128))
    sums = jnp.zeros((ROWS, 128), f32)
    for k in range(8):
        sums = sums + jnp.where(index[k : k + 1] == site, stock[k : k + 1], 0.0)
    column = jnp.sum(sums, axis=1, keepdims=True)
    as_row = jnp.sum(jnp.where(lanes_of((ROWS, 128)) == site, column, 0.0), axis=0, keepdims=True)
    base = stock - learn_rate * (hold_ref[...] + mult_ref[...])
    low = lanes_of((ROWS, 128)) < SCEN
    for q in range(Y):
        tile = slice(q // 2 * 128, q // 2 * 128 + 128)
        rec = rec_ref[:, tile]
        short = demand_ref[:, tile].astype(f32) - column
        if q % 2 == 0:
            both = jnp.where(low, rec, pltpu.roll(short, SCEN, 1))
        else:
            both = jnp.where(low, pltpu.roll(rec, SCEN, 1), short)
        packed_ref[q * ROWS : (q + 1) * ROWS, :] = both
    packed_ref[Y * ROWS : Y * ROWS + 8, :] = base
    packed_ref[Y * ROWS + 8 : Y * ROWS + 16, :] = index.astype(f32)
    packed_ref[Y * ROWS + 16 : Y * ROWS + 24, :] = jnp.broadcast_to(as_row, (8, 128))


def spread_z_kernel(place_ref, packed_ref, transship_ref, spread_ref):
    at = pl.ds(pl.multiple_of(place_ref[3] * COLS, COLS), COLS)
    block = transship_ref[:, at]
    for z in range(Z):
        spread_ref[z] = block


def recourse_steps(core, mine_ref, other_ref, rec_ref, short_ref, grad_ref, rounded_ref):
    def one_step(inner, carry):
        square = jnp.zeros((ROWS, 128), f32)
        for y in range(Y):
            acc = jnp.zeros((512, 128), f32)
            for x in range(X):
                for ref, chunk in ((mine_ref, 2 * x + core), (other_ref, 2 * x + 1 - core)):
                    at = pl.ds(pl.multiple_of(chunk * COLS, COLS), COLS)
                    acc = acc + jnp.dot(
                        ref[x * Y + y], rounded_ref[at, :], preferred_element_type=f32
                    )
            for z in range(Z):
                at = pl.ds((z * Y + y) * ROWS, ROWS)
                grad = acc[z * ROWS : (z + 1) * ROWS] - penalty * (short_ref[at, :] - rec_ref[at, :])
                grad_ref[at, :] = grad
                square = square + grad * grad
        square = jnp.sum(square, axis=0, keepdims=True)
        factor = stride / jnp.sqrt(square / SITE_COUNT + epsilon)

        def renew(j, carry):
            at = pl.ds(pl.multiple_of(j * 256, 256), 256)
            rec = jnp.maximum(rec_ref[at, :] - grad_ref[at, :] * factor, 0.0)
            rec_ref[at, :] = rec
            rounded_ref[at, :] = rec.astype(jnp.bfloat16)
            return carry

        lax.fori_loop(0, 8, renew, 0)
        return carry

    lax.fori_loop(0, 2, one_step, 0)


def pull_sums(share, rec_ref, short_ref, put):
    for z in range(Z):
        at = pl.ds(z * 128, 128)
        gap = penalty * (short_ref[at, :] - rec_ref[at, :]) * share
        put(z, jnp.sum(gap.T, axis=0, keepdims=True))


def arrange_kernel(place_ref, gathered_ref, sites_ref, parts_ref, sums_ref, padded_ref, sems):
    started = [
        pltpu.make_async_copy(
            gathered_ref.at[:, pl.ds(q * ROWS, ROWS), :], sites_ref.at[q], sems.at[q]
        )
        for q in range(Y)
    ]
    start = Y * ROWS
    started.append(
        pltpu.make_async_copy(gathered_ref.at[:, pl.ds(start, 16), :], parts_ref, sems.at[Y])
    )
    started.append(
        pltpu.make_async_copy(gathered_ref.at[:, pl.ds(start + 16, 8), :], padded_ref, sems.at[Y + 1])
    )
    for copy in started:
        copy.start()
    for copy in started:
        copy.wait()
    for z in range(Z):
        sums_ref[z : z + 1, :] = padded_ref[z, 0:1, :]


def first_kernel(
    place_ref,
    aux_ref,
    mine_ref,
    other_ref,
    sites_ref,
    parts_ref,
    sums_ref,
    rec_ref,
    short_ref,
    middle_ref,
    grad_ref,
    rounded_ref,
):
    def load(b, carry):
        at = pl.ds(pl.multiple_of(b * ROWS, ROWS), ROWS)
        both = sites_ref[b % Y, b // Y]
        rec_ref[at, :] = both
        rounded_ref[at, :] = both.astype(jnp.bfloat16)
        short_ref[at, :] = pltpu.roll(both, SCEN, 1)
        return carry

    lax.fori_loop(0, Z * Y, load, 0, unroll=8)
    recourse_steps(place_ref[0], mine_ref, other_ref, rec_ref, short_ref, grad_ref, rounded_ref)

    def put(z, row):
        for q in range(Y):
            middle_ref[q, z : z + 1, :] = row
            middle_ref[q, Z + z * 16 : Z + z * 16 + 16, :] = parts_ref[z]

    pull_sums(aux_ref[0:1, :], rec_ref, short_ref, put)
    for q in range(Y):
        middle_ref[q, MIDDLE - Z : MIDDLE, :] = sums_ref[...]


def second_kernel(
    place_ref,
    aux_ref,
    mine_ref,
    other_ref,
    middle_ref,
    rec_in_ref,
    short_in_ref,
    mult_ref,
    send_ref,
    rec_ref,
    pull_ref,
    short_ref,
    grad_ref,
    rounded_ref,
):
    pull_ref[0] = middle_ref[0, 0:Z] + middle_ref[1, 0:Z] + middle_ref[2, 0:Z] + middle_ref[3, 0:Z]
    eye = lanes_of((ROWS, 128)) == rows_of((ROWS, 128))
    site = rows_of((ROWS, 128)).astype(f32)

    def load(b, carry):
        at = pl.ds(pl.multiple_of(b * ROWS, ROWS), ROWS)
        z, y = b // Y, b % Y
        start = pl.multiple_of(Z + z * 16, 8)
        index = middle_ref[y, pl.ds(start + 8, 8), :]
        pull = pick(pull_ref[0, pl.ds(z, 1), :], index.astype(jnp.int32) + y * ROWS)
        stock = jnp.maximum(middle_ref[y, pl.ds(start, 8), :] + learn_rate * pull, 0.0)
        change = jnp.where(eye, -middle_ref[y, pl.ds(MIDDLE - Z + z, 1), :], 0.0)
        for k in range(8):
            change = change + jnp.where(index[k : k + 1] == site, stock[k : k + 1], 0.0)
        rec = rec_in_ref[at, :]
        rec_ref[at, :] = rec
        rounded_ref[at, :] = rec.astype(jnp.bfloat16)
        short_ref[at, :] = short_in_ref[at, :] - jnp.sum(change, axis=1, keepdims=True)
        return carry

    lax.fori_loop(0, Z * Y, load, 0, unroll=8)
    recourse_steps(place_ref[0], mine_ref, other_ref, rec_ref, short_ref, grad_ref, rounded_ref)

    def put(z, row):
        pull_ref[1, z : z + 1, :] = row

    pull_sums(aux_ref[0:1, :], rec_ref, short_ref, put)
    z = place_ref[1]
    sub = rows_of((8, 128))
    pulls = jnp.where(
        sub == 0,
        pull_ref[0, pl.ds(z, 1), :],
        jnp.where(sub == 1, pull_ref[1, pl.ds(z, 1), :], aux_ref[8:9, :]),
    )
    low = lanes_of((16, 128)) < SCEN
    for q in range(Y):
        start = pl.multiple_of((z * Y + q) * ROWS, ROWS)
        upper = rec_ref[pl.ds(start, 16), :]
        lower = rec_ref[pl.ds(start + 16, 16), :]
        pair = jnp.where(low, upper, pltpu.roll(lower, SCEN, 1))
        for g in range(GROUPS):
            send_ref[g * Y + q, 0:8, :] = mult_ref[...]
            send_ref[g * Y + q, 8:16, :] = pulls
            send_ref[g * Y + q, 16:32, :] = pair


def last_kernel(
    place_ref, got_ref, assign_ref, hold_ref, stock_ref, consensus_ref, mult_ref, rec_ref, all_ref
):
    z, y, column = place_ref[1], place_ref[2], place_ref[3]
    index = assign_ref[...] - z * (Y * ROWS)
    hold = hold_ref[...]
    start = stock_ref[...]
    totals = [got_ref[g * Y, 10:11, :] for g in range(GROUPS)]
    all_total = totals[0]
    for g in range(1, GROUPS):
        all_total = all_total + totals[g]
    mults = [got_ref[g * Y + y, 0:8, :] for g in range(GROUPS)]
    stocks = []
    weighted = jnp.zeros((8, 128), f32)
    for g in range(GROUPS):
        pull = pick(got_ref[g * Y, 8:9, :], index)
        stock = jnp.maximum(start - learn_rate * (hold + mults[g] - pull), 0.0)
        weighted = weighted + totals[g] * stock
        stocks.append(stock)
    consensus = weighted / all_total
    weighted = jnp.zeros((8, 128), f32)
    for g in range(GROUPS):
        row = got_ref[g * Y, 9:10, :]
        for q in range(1, Y):
            row = row + got_ref[g * Y + q, 9:10, :]
        pull = pick(row, index)
        apart = prox_weight * (stocks[g] - consensus)
        mults[g] = mults[g] + apart
        stock = jnp.maximum(stocks[g] - learn_rate * (hold + mults[g] - pull + apart), 0.0)
        weighted = weighted + totals[g] * stock
        stocks[g] = stock
    consensus = weighted / all_total
    consensus_ref[...] = consensus
    for g in range(GROUPS):
        all_ref[g] = mults[g] + prox_weight * (stocks[g] - consensus)
    mult_ref[...] = all_ref[column]

    low = lanes_of((16, 128)) < SCEN
    for m in range(2):
        tile = slice(m * 128, m * 128 + 128)
        even = got_ref[column * Y + 2 * m, 16:32, :]
        odd = got_ref[column * Y + 2 * m + 1, 16:32, :]
        rec_ref[0:16, tile] = jnp.where(low, even, pltpu.roll(odd, SCEN, 1))
        rec_ref[16:32, tile] = jnp.where(low, pltpu.roll(even, SCEN, 1), odd)


def run_kernel(kernel, outs, scratch, *args, hbm=0, vmem_mib=16, flops=0):
    vmem = pl.BlockSpec(memory_space=pltpu.VMEM)
    outs = [out if isinstance(out, jax.ShapeDtypeStruct) else jax.ShapeDtypeStruct(out, f32) for out in outs]
    return pl.pallas_call(
        kernel,
        out_shape=outs,
        in_specs=[pl.BlockSpec(memory_space=pltpu.SMEM)]
        + [pl.BlockSpec(memory_space=pl.ANY)] * hbm
        + [vmem] * (len(args) - 1 - hbm),
        out_specs=[vmem] * len(outs),
        scratch_shapes=[pltpu.VMEM(*entry) if isinstance(entry, tuple) else entry for entry in scratch],
        cost_estimate=pl.CostEstimate(flops=flops, bytes_accessed=0, transcendentals=0) if flops else None,
        compiler_params=pltpu.CompilerParams(vmem_limit_bytes=vmem_mib * 1024 * 1024),
    )(*args)


def one_block(always, work, *args):
    shapes = jax.eval_shape(work, *args)

    def never(*args):
        return jax.tree.map(lambda shape: jnp.zeros(shape.shape, shape.dtype), shapes)

    return lax.cond(always, work, never, *args)


def per_device(demand, recourse_init, transship, counts, assign, hold_cost, stock_init, mult_init):
    core = lax.axis_index("core")
    column = lax.axis_index("x") * CORE + core
    y = lax.axis_index("y")
    z = lax.axis_index("z")
    place = jnp.stack([core, z, y, column]).astype(jnp.int32)
    wide = (SITE_COUNT, 128)
    assign = assign.reshape(8, 128)
    hold_cost = hold_cost.reshape(8, 128)
    stock_init = stock_init.reshape(8, 128)
    mult_init = mult_init.reshape(8, 128)

    raw = (
        demand,
        recourse_init,
        counts.reshape(2, 128),
        assign,
        hold_cost,
        stock_init,
        mult_init,
    )
    packed, aux = run_kernel(
        prep_kernel,
        [(Y * ROWS + PARTS, 128), (16, 128)],
        [(entry.shape, entry.dtype) for entry in raw] + [pltpu.SemaphoreType.DMA((7,))],
        place,
        *raw,
        hbm=len(raw),
        vmem_mib=60,
    )
    bf16 = jnp.bfloat16
    always = column * COLS >= 0

    def spread_z(transship, packed):
        (block,) = run_kernel(
            spread_z_kernel,
            [jax.ShapeDtypeStruct((Z, ROWS, COLS), bf16)],
            [],
            place,
            packed,
            transship,
            hbm=1,
        )
        return lax.all_to_all(block, "z", 0, 0, tiled=True).reshape(Z * ROWS, COLS)

    def spread_xy(along_z):
        spread = jnp.broadcast_to(along_z[None], (X * Y, Z * ROWS, COLS))
        return lax.all_to_all(spread, ("x", "y"), 0, 0, tiled=True)

    gathered = lax.all_gather(packed, "z", axis=0)
    along_z = one_block(always, spread_z, transship, packed)
    mine = one_block(always, spread_xy, along_z)
    sites, parts, sums = run_kernel(
        arrange_kernel,
        [(Y, Z, ROWS, 128), (Z, 16, 128), (Z, 128)],
        [((Z, 8, 128), f32), pltpu.SemaphoreType.DMA((Y + 2,))],
        place,
        gathered,
        hbm=1,
        vmem_mib=16,
        flops=0,
    )

    def exchange(mine, sites):
        other = lax.ppermute(mine, "core", [(0, 1), (1, 0)])
        return other, lax.all_to_all(sites, "y", 0, 0, tiled=True)

    other, sites = one_block(always, exchange, mine, sites)
    rec, short, middle = run_kernel(
        first_kernel,
        [wide, wide, (Y, MIDDLE, 128)],
        [(wide, f32), (wide, bf16)],
        place,
        aux,
        mine,
        other,
        sites,
        parts,
        sums,
    )
    middle = lax.all_to_all(middle, "y", 0, 0, tiled=True)
    (send,) = run_kernel(
        second_kernel,
        [(GROUPS * Y, 32, 128)],
        [(wide, f32), ((2, Z, 128), f32), (wide, f32), (wide, f32), (wide, jnp.bfloat16)],
        place,
        aux,
        mine,
        other,
        middle,
        rec,
        short,
        mult_init,
    )
    got = lax.all_to_all(send, ("x", "core", "y"), 0, 0, tiled=True)
    consensus, multipliers, recourse = run_kernel(
        last_kernel,
        [(8, 128), (8, 128), (ROWS, Y * SCEN)],
        [((GROUPS, 8, 128), f32)],
        place,
        got,
        assign,
        hold_cost,
        stock_init,
    )
    return (consensus.reshape(1024), multipliers.reshape(1, 1024), recourse)


def solution(mesh):
    grid = Mesh(mesh.devices.reshape(X, CORE, Z, Y), ("x", "core", "z", "y"))
    scen, dom = ("x", "core"), ("z", "y")
    in_specs = (
        P(dom, scen),
        P(dom, scen),
        P(dom, None),
        P(scen),
        P(dom),
        P(dom),
        P(dom),
        P(scen, dom),
    )
    out_specs = (P(dom), P(scen, dom), P(dom, scen))
    return jax.shard_map(
        per_device, mesh=grid, in_specs=in_specs, out_specs=out_specs, check_vma=False
    )
```

```python
import jax
import jax.numpy as jnp
from jax import lax
from jax.experimental import pallas as pl
from jax.experimental.pallas import tpu as pltpu
from jax.sharding import Mesh, PartitionSpec as P

SITE_COUNT = 2048
X, CORE, Z, Y = 4, 2, 16, 4
GROUPS = X * CORE
ROWS = 32
COLS = 256
SCEN = 16
HALF = 64
BLOCK = 64
LOCAL = 48

penalty = 1.0
stride = 0.5
prox_weight = 2.0
learn_rate = 0.05
epsilon = 1e-05

f32, bf16 = jnp.float32, jnp.bfloat16


def lanes_of(shape):
    return lax.broadcasted_iota(jnp.int32, shape, len(shape) - 1)


def rows_of(shape):
    return lax.broadcasted_iota(jnp.int32, shape, len(shape) - 2)


def pick(row, index):
    return jnp.take_along_axis(
        jnp.broadcast_to(row, (8, 128)), index, axis=1, mode="promise_in_bounds"
    )


def narrow(value):
    return value.astype(bf16).astype(f32)


def turn(value, shift):
    return pltpu.roll(value, shift % 128, len(value.shape) - 1)


def prep_kernel(place_ref, transship_ref, *refs):
    inputs, (send_ref, aux_ref), copies = refs[:7], refs[7:9], refs[9:16]
    block_ref, sems = refs[16], refs[17]
    z, y, column = place_ref[1], place_ref[2], place_ref[3]
    at = pl.ds(pl.multiple_of(column * COLS, COLS), COLS)
    started = [
        pltpu.make_async_copy(source, target, sems.at[k])
        for k, (source, target) in enumerate(zip(inputs, copies))
    ]
    started.append(pltpu.make_async_copy(transship_ref.at[:, at], block_ref, sems.at[7]))
    for copy in started:
        copy.start()
    for copy in started:
        copy.wait()
    demand_ref, rec_ref, counts_ref, assign_ref, hold_ref, stock_ref, mult_ref = copies

    weights = counts_ref[...].astype(f32)
    total = jnp.sum(jnp.sum(weights, axis=1, keepdims=True), axis=0, keepdims=True)
    row = jnp.broadcast_to(jnp.where(z >= 8, weights[1:2], weights[0:1]) / total, (8, 128))
    row = pltpu.roll(row, (128 - z % 8 * SCEN) % 128, 1)
    aux_ref[0:8, :] = jnp.where(lanes_of((8, 128)) < SCEN, row, 0.0)
    aux_ref[8:16, :] = jnp.broadcast_to(total, (8, 128))

    index = assign_ref[...] - (z * Y + y) * ROWS
    stock = stock_ref[...]
    site = rows_of((ROWS, 128))
    lane = lanes_of((ROWS, 128))
    sums = jnp.zeros((ROWS, 128), f32)
    for k in range(8):
        sums = sums + jnp.where(index[k : k + 1] == site, stock[k : k + 1], 0.0)
    column_sum = jnp.sum(sums, axis=1, keepdims=True)
    high = narrow(column_sum)
    middle = narrow(column_sum - high)
    spread = jnp.where(lane == site, high, 0.0)
    spread = jnp.where(lane == site + ROWS, middle, spread)
    spread = jnp.where(lane == site + 2 * ROWS, column_sum - high - middle, spread)
    sum_row = jnp.broadcast_to(jnp.sum(spread, axis=0, keepdims=True), (8, 128))
    base = stock - learn_rate * (hold_ref[...] + mult_ref[...])
    parts = jnp.concatenate([narrow(base), base - narrow(base), index.astype(f32), sum_row], axis=0)
    parts = parts.astype(bf16)
    for n in range(Z):
        tile = slice(n // 8 * 128, n // 8 * 128 + 128)
        at = n % 8 * SCEN
        rec = rec_ref[:, tile]
        rounded = narrow(rec)
        both = jnp.where(
            lane < SCEN,
            turn(rounded, -at),
            jnp.where(
                lane < 2 * SCEN,
                turn(rec - rounded, SCEN - at),
                turn(demand_ref[:, tile].astype(f32), 2 * SCEN - at),
            ),
        )
        both = jnp.where(lane[0:16] < HALF, both[0:16], turn(both[16:32], HALF))
        send_ref[n, 0:ROWS, :] = block_ref[:, 0:128]
        send_ref[n, ROWS:BLOCK, :] = block_ref[:, 128:256]
        send_ref[n, BLOCK : BLOCK + 16, :] = both.astype(bf16)
        send_ref[n, BLOCK + 16 : BLOCK + LOCAL, :] = parts


def spread_kernel(place_ref, got_ref, spread_ref, local_ref):
    for z in range(Z):
        local_ref[z] = got_ref[z, BLOCK:, :]

    def put(n, carry):
        for z in range(Z):
            spread_ref[n, z * ROWS : (z + 1) * ROWS, 0:128] = got_ref[z, 0:ROWS, :]
            spread_ref[n, z * ROWS : (z + 1) * ROWS, 128:256] = got_ref[z, ROWS:BLOCK, :]
        return carry

    lax.fori_loop(0, X * Y, put, 0)


def repeat_kernel(place_ref, mine_ref, local_ref, send_ref):
    for q in range(Y):
        send_ref[q] = local_ref[...]


def recourse_steps(core, mine_ref, other_ref, rec_ref, short_ref, grad_ref, rounded_ref):
    def one_step(inner, carry):
        square = jnp.zeros((ROWS, 128), f32)
        for y in range(Y):
            acc = jnp.zeros((512, 128), f32)
            for x in range(X):
                for ref, chunk in ((mine_ref, 2 * x + core), (other_ref, 2 * x + 1 - core)):
                    at = pl.ds(pl.multiple_of(chunk * COLS, COLS), COLS)
                    acc = acc + jnp.dot(
                        ref[x * Y + y], rounded_ref[at, :], preferred_element_type=f32
                    )
            for z in range(Z):
                at = pl.ds((z * Y + y) * ROWS, ROWS)
                grad = acc[z * ROWS : (z + 1) * ROWS] - penalty * (short_ref[at, :] - rec_ref[at, :])
                grad_ref[at, :] = grad
                square = square + grad * grad
        square = jnp.sum(square, axis=0, keepdims=True)
        factor = stride / jnp.sqrt(square / SITE_COUNT + epsilon)

        def renew(j, carry):
            at = pl.ds(pl.multiple_of(j * 256, 256), 256)
            rec = jnp.maximum(rec_ref[at, :] - grad_ref[at, :] * factor, 0.0)
            rec_ref[at, :] = rec
            rounded_ref[at, :] = rec.astype(jnp.bfloat16)
            return carry

        lax.fori_loop(0, 8, renew, 0)
        return carry

    lax.fori_loop(0, 2, one_step, 0)


def pull_sums(share, rec_ref, short_ref, put):
    for z in range(Z):
        at = pl.ds(z * 128, 128)
        gap = penalty * (short_ref[at, :] - rec_ref[at, :]) * share
        put(z, jnp.sum(gap.T, axis=0, keepdims=True))


def first_kernel(
    place_ref, aux_ref, mine_ref, other_ref, local_ref, rec_ref, short_ref, pull_ref, grad_ref, rounded_ref
):
    lane, sub = lanes_of((ROWS, 128)), rows_of((ROWS, 128))
    picked = (lane % ROWS == sub) & (lane < 3 * ROWS)

    def load(b, carry):
        at = pl.ds(pl.multiple_of(b * ROWS, ROWS), ROWS)
        local = local_ref[b % Y, b // Y].astype(f32)
        both = jnp.concatenate([local[0:16], turn(local[0:16], HALF)], axis=0)
        rec = both + turn(both, -SCEN)
        old = jnp.sum(jnp.where(picked, local[40:41], 0.0), axis=1, keepdims=True)
        rec_ref[at, :] = rec
        rounded_ref[at, :] = rec.astype(bf16)
        short_ref[at, :] = turn(both, -2 * SCEN) - old
        return carry

    lax.fori_loop(0, Z * Y, load, 0, unroll=8)
    recourse_steps(place_ref[0], mine_ref, other_ref, rec_ref, short_ref, grad_ref, rounded_ref)

    def put(z, row):
        for n in range(Z):
            pull_ref[n, z : z + 1, :] = row

    pull_sums(aux_ref[0:1, :], rec_ref, short_ref, put)


def second_kernel(
    place_ref,
    aux_ref,
    mine_ref,
    other_ref,
    local_ref,
    rec_in_ref,
    short_in_ref,
    pulled_ref,
    send_ref,
    own_ref,
    rec_ref,
    pull_ref,
    short_ref,
    grad_ref,
    rounded_ref,
):
    total = pulled_ref[0]
    for n in range(1, Z):
        total = total + pulled_ref[n]
    pull_ref[0] = total
    lane, sub = lanes_of((ROWS, 128)), rows_of((ROWS, 128))
    picked = (lane % ROWS == sub) & (lane < 3 * ROWS)
    site = sub.astype(f32)

    def load(b, carry):
        at = pl.ds(pl.multiple_of(b * ROWS, ROWS), ROWS)
        local = local_ref[b % Y, b // Y, 16:48, :].astype(f32)
        index = local[16:24]
        pull = pick(pull_ref[0, pl.ds(b // Y, 1), :], index.astype(jnp.int32) + b % Y * ROWS)
        stock = jnp.maximum(local[0:8] + local[8:16] + learn_rate * pull, 0.0)
        change = jnp.where(picked, -local[24:25], 0.0)
        for k in range(8):
            change = change + jnp.where(index[k : k + 1] == site, stock[k : k + 1], 0.0)
        rec = rec_in_ref[at, :]
        rec_ref[at, :] = rec
        rounded_ref[at, :] = rec.astype(bf16)
        short_ref[at, :] = short_in_ref[at, :] - jnp.sum(change, axis=1, keepdims=True)
        return carry

    lax.fori_loop(0, Z * Y, load, 0, unroll=8)
    recourse_steps(place_ref[0], mine_ref, other_ref, rec_ref, short_ref, grad_ref, rounded_ref)

    def put(z, row):
        pull_ref[1, z : z + 1, :] = row

    pull_sums(aux_ref[0:1, :], rec_ref, short_ref, put)
    z, y = place_ref[1], place_ref[2]
    back = (128 - y * ROWS) % 128
    own_ref[...] = pltpu.roll(jnp.broadcast_to(pull_ref[0, pl.ds(z, 1), :], (8, 128)), back, 1)
    lane = lanes_of((8, 128))
    for n in range(Z):
        start = pl.multiple_of((n * Y + y) * ROWS, ROWS)
        pull = pltpu.roll(jnp.broadcast_to(pull_ref[1, n : n + 1, :], (8, 128)), back, 1)
        block = turn(pull, 4 * SCEN)
        for k in range(3, -1, -1):
            rows = rec_ref[pl.ds(start + 8 * k, 8), :]
            block = jnp.where(lane < (k + 1) * SCEN, turn(rows, k * SCEN), block)
        send_ref[n] = block


def fold_kernel(place_ref, got_ref, own_ref, aux_ref, mult_ref, rec_ref, send_ref):
    lane, sub = lanes_of((8, 128)), rows_of((8, 128))
    pull = got_ref[0]
    for n in range(1, Z):
        pull = pull + got_ref[n]
    pull = jnp.broadcast_to(turn(pull, -4 * SCEN)[0:1], (8, 128))
    pulls = jnp.where(sub == 0, own_ref[...], jnp.where(sub == 1, pull, aux_ref[8:16, :]))
    for g in range(GROUPS):
        send_ref[g, 0:8, :] = mult_ref[...]
        send_ref[g, 8:16, :] = pulls
    for m in range(2):
        for k in range(4):
            out = turn(got_ref[8 * m], -k * SCEN)
            for n in range(1, 8):
                moved = turn(got_ref[8 * m + n], (n - k) * SCEN)
                out = jnp.where(lane < n * SCEN, out, moved)
            rec_ref[8 * k : 8 * k + 8, m * 128 : m * 128 + 128] = out


def last_kernel(place_ref, got_ref, assign_ref, hold_ref, stock_ref, consensus_ref, mult_ref, all_ref):
    z, y, column = place_ref[1], place_ref[2], place_ref[3]
    index = assign_ref[...] - (z * Y + y) * ROWS
    hold = hold_ref[...]
    start = stock_ref[...]
    totals = [got_ref[g, 10:11, :] for g in range(GROUPS)]
    all_total = totals[0]
    for g in range(1, GROUPS):
        all_total = all_total + totals[g]
    mults = [got_ref[g, 0:8, :] for g in range(GROUPS)]
    stocks = []
    weighted = jnp.zeros((8, 128), f32)
    for g in range(GROUPS):
        pull = pick(got_ref[g, 8:9, :], index)
        stock = jnp.maximum(start - learn_rate * (hold + mults[g] - pull), 0.0)
        weighted = weighted + totals[g] * stock
        stocks.append(stock)
    consensus = weighted / all_total
    weighted = jnp.zeros((8, 128), f32)
    for g in range(GROUPS):
        pull = pick(got_ref[g, 9:10, :], index)
        apart = prox_weight * (stocks[g] - consensus)
        mults[g] = mults[g] + apart
        stock = jnp.maximum(stocks[g] - learn_rate * (hold + mults[g] - pull + apart), 0.0)
        weighted = weighted + totals[g] * stock
        stocks[g] = stock
    consensus = weighted / all_total
    consensus_ref[...] = consensus
    for g in range(GROUPS):
        all_ref[g] = mults[g] + prox_weight * (stocks[g] - consensus)
    mult_ref[...] = all_ref[column]


def run_kernel(kernel, outs, scratch, *args, hbm=0, vmem_mib=16):
    vmem = pl.BlockSpec(memory_space=pltpu.VMEM)
    return pl.pallas_call(
        kernel,
        out_shape=[jax.ShapeDtypeStruct(*out) for out in outs],
        in_specs=[pl.BlockSpec(memory_space=pltpu.SMEM)]
        + [pl.BlockSpec(memory_space=pl.ANY)] * hbm
        + [vmem] * (len(args) - 1 - hbm),
        out_specs=[vmem] * len(outs),
        scratch_shapes=[pltpu.VMEM(*entry) if isinstance(entry, tuple) else entry for entry in scratch],
        compiler_params=pltpu.CompilerParams(vmem_limit_bytes=vmem_mib * 1024 * 1024),
    )(*args)


def per_device(demand, recourse_init, transship, counts, assign, hold_cost, stock_init, mult_init):
    core = lax.axis_index("core")
    column = lax.axis_index("x") * CORE + core
    y = lax.axis_index("y")
    z = lax.axis_index("z")
    place = jnp.stack([core, z, y, column]).astype(jnp.int32)
    wide = ((SITE_COUNT, 128), f32)
    wide16 = ((SITE_COUNT, 128), bf16)
    tile = ((8, 128), f32)
    assign = assign.reshape(8, 128)
    hold_cost = hold_cost.reshape(8, 128)
    stock_init = stock_init.reshape(8, 128)
    mult_init = mult_init.reshape(8, 128)

    raw = (
        demand,
        recourse_init,
        counts.reshape(2, 128),
        assign,
        hold_cost,
        stock_init,
        mult_init,
    )
    send, aux = run_kernel(
        prep_kernel,
        [((Z, BLOCK + LOCAL, 128), bf16), ((16, 128), f32)],
        [(entry.shape, entry.dtype) for entry in raw]
        + [((ROWS, COLS), bf16), pltpu.SemaphoreType.DMA((8,))],
        place,
        transship,
        *raw,
        hbm=8,
        vmem_mib=60,
    )
    got = lax.all_to_all(send, "z", 0, 0, tiled=True)
    spread, local = run_kernel(
        spread_kernel,
        [((X * Y, Z * ROWS, COLS), bf16), ((Z, LOCAL, 128), bf16)],
        [],
        place,
        got,
    )
    mine = lax.all_to_all(spread, ("x", "y"), 0, 0, tiled=True)
    other = lax.ppermute(mine, "core", [(0, 1), (1, 0)])
    (local,) = run_kernel(repeat_kernel, [((Y, Z, LOCAL, 128), bf16)], [], place, mine, local, hbm=1)
    local = lax.all_to_all(local, "y", 0, 0, tiled=True)

    rec, short, pull = run_kernel(
        first_kernel,
        [wide, wide, ((Z, Z, 128), f32)],
        [wide, wide16],
        place,
        aux,
        mine,
        other,
        local,
    )
    pull = lax.all_to_all(pull, "z", 0, 0, tiled=True)
    send, own = run_kernel(
        second_kernel,
        [((Z, 8, 128), f32), tile],
        [wide, ((2, Z, 128), f32), wide, wide, wide16],
        place,
        aux,
        mine,
        other,
        local,
        rec,
        short,
        pull,
    )
    got = lax.all_to_all(send, "z", 0, 0, tiled=True)
    recourse, send = run_kernel(
        fold_kernel,
        [((ROWS, Z * SCEN), f32), ((GROUPS, 16, 128), f32)],
        [],
        place,
        got,
        own,
        aux,
        mult_init,
    )
    got = lax.all_to_all(send, ("x", "core"), 0, 0, tiled=True)
    consensus, multipliers = run_kernel(
        last_kernel,
        [tile, tile],
        [((GROUPS, 8, 128), f32)],
        place,
        got,
        assign,
        hold_cost,
        stock_init,
    )
    return (consensus.reshape(1024), multipliers.reshape(1, 1024), recourse)


def solution(mesh):
    grid = Mesh(mesh.devices.reshape(X, CORE, Z, Y), ("x", "core", "z", "y"))
    scen, dom = ("x", "core"), ("z", "y")
    in_specs = (
        P(dom, scen),
        P(dom, scen),
        P(dom, None),
        P(scen),
        P(dom),
        P(dom),
        P(dom),
        P(scen, dom),
    )
    out_specs = (P(dom), P(scen, dom), P(dom, scen))
    return jax.shard_map(
        per_device, mesh=grid, in_specs=in_specs, out_specs=out_specs, check_vma=False
    )
```

```python
import jax
import jax.numpy as jnp
from jax import lax
from jax.experimental import pallas as pl
from jax.experimental.pallas import tpu as pltpu
from jax.sharding import Mesh, PartitionSpec as P

SITE_COUNT = 2048
X, CORE, Z, Y = 4, 2, 16, 4
GROUPS = X * CORE
ROWS = 32
COLS = 256
SCEN = 64
PARTS = 24

penalty = 1.0
stride = 0.5
prox_weight = 2.0
learn_rate = 0.05
epsilon = 1e-05

f32 = jnp.float32


def lanes_of(shape):
    return lax.broadcasted_iota(jnp.int32, shape, len(shape) - 1)


def rows_of(shape):
    return lax.broadcasted_iota(jnp.int32, shape, len(shape) - 2)


def pick(row, index):
    return jnp.take_along_axis(
        jnp.broadcast_to(row, (8, 128)), index, axis=1, mode="promise_in_bounds"
    )


def prep_kernel(place_ref, transship_ref, *refs):
    inputs, (packed_ref, aux_ref, spread_ref), copies = refs[:7], refs[7:10], refs[10:17]
    block_ref, sems = refs[17], refs[18]
    at = pl.ds(pl.multiple_of(place_ref[3] * COLS, COLS), COLS)
    started = [
        pltpu.make_async_copy(source, target, sems.at[k])
        for k, (source, target) in enumerate(zip(inputs, copies))
    ]
    started.append(pltpu.make_async_copy(transship_ref.at[:, at], block_ref, sems.at[7]))
    for copy in started:
        copy.start()
    for copy in started:
        copy.wait()
    demand_ref, rec_ref, counts_ref, assign_ref, hold_ref, stock_ref, mult_ref = copies
    for n in range(Z):
        spread_ref[n] = block_ref[...]
    z, y = place_ref[1], place_ref[2]
    weights = counts_ref[...].astype(f32)
    total = jnp.sum(jnp.sum(weights, axis=1, keepdims=True), axis=0, keepdims=True)
    row = jnp.where(y >= 2, weights[1:2], weights[0:1])
    row = jnp.where(y % 2 == 1, pltpu.roll(row, SCEN, 1), row) / total
    row = jnp.where(lanes_of((1, 128)) < SCEN, row, 0.0)
    aux_ref[0:8, :] = jnp.broadcast_to(row, (8, 128))
    aux_ref[8:16, :] = jnp.broadcast_to(total, (8, 128))

    index = assign_ref[...] - (z * Y + y) * ROWS
    stock = stock_ref[...]
    site = rows_of((ROWS, 128))
    sums = jnp.zeros((ROWS, 128), f32)
    for k in range(8):
        sums = sums + jnp.where(index[k : k + 1] == site, stock[k : k + 1], 0.0)
    column = jnp.sum(sums, axis=1, keepdims=True)
    as_row = jnp.sum(jnp.where(lanes_of((ROWS, 128)) == site, column, 0.0), axis=0, keepdims=True)
    base = stock - learn_rate * (hold_ref[...] + mult_ref[...])
    low = lanes_of((ROWS, 128)) < SCEN
    for q in range(Y):
        tile = slice(q // 2 * 128, q // 2 * 128 + 128)
        rec = rec_ref[:, tile]
        short = demand_ref[:, tile].astype(f32) - column
        if q % 2 == 0:
            both = jnp.where(low, rec, pltpu.roll(short, SCEN, 1))
        else:
            both = jnp.where(low, pltpu.roll(rec, SCEN, 1), short)
        packed_ref[q, 0:ROWS, :] = both
        packed_ref[q, ROWS : ROWS + 8, :] = base
        packed_ref[q, ROWS + 8 : ROWS + 16, :] = index.astype(f32)
        packed_ref[q, ROWS + 16 : ROWS + 24, :] = jnp.broadcast_to(as_row, (8, 128))


def recourse_steps(core, mine_ref, other_ref, rec_ref, short_ref, grad_ref, rounded_ref):
    def one_step(inner, carry):
        square = jnp.zeros((ROWS, 128), f32)
        for y in range(Y):
            acc = jnp.zeros((512, 128), f32)
            for x in range(X):
                for ref, chunk in ((mine_ref, 2 * x + core), (other_ref, 2 * x + 1 - core)):
                    at = pl.ds(pl.multiple_of(chunk * COLS, COLS), COLS)
                    acc = acc + jnp.dot(
                        ref[x * Y + y], rounded_ref[at, :], preferred_element_type=f32
                    )
            for z in range(Z):
                at = pl.ds((z * Y + y) * ROWS, ROWS)
                grad = acc[z * ROWS : (z + 1) * ROWS] - penalty * (short_ref[at, :] - rec_ref[at, :])
                grad_ref[at, :] = grad
                square = square + grad * grad
        square = jnp.sum(square, axis=0, keepdims=True)
        factor = stride / jnp.sqrt(square / SITE_COUNT + epsilon)

        def renew(j, carry):
            at = pl.ds(pl.multiple_of(j * 256, 256), 256)
            rec = jnp.maximum(rec_ref[at, :] - grad_ref[at, :] * factor, 0.0)
            rec_ref[at, :] = rec
            rounded_ref[at, :] = rec.astype(jnp.bfloat16)
            return carry

        lax.fori_loop(0, 8, renew, 0)
        return carry

    lax.fori_loop(0, 2, one_step, 0)


def pull_sums(share, rec_ref, short_ref, put):
    for z in range(Z):
        at = pl.ds(z * 128, 128)
        gap = penalty * (short_ref[at, :] - rec_ref[at, :]) * share
        put(z, jnp.sum(gap.T, axis=0, keepdims=True))


def unpack_kernel(place_ref, packed_ref, rec_ref, short_ref):
    def load(b, carry):
        at = pl.ds(pl.multiple_of(b * ROWS, ROWS), ROWS)
        both = packed_ref[b, 0:ROWS, :]
        rec_ref[at, :] = both
        short_ref[at, :] = pltpu.roll(both, SCEN, 1)
        return carry

    lax.fori_loop(0, Z * Y, load, 0, unroll=8)


def first_kernel(
    place_ref, aux_ref, mine_ref, other_ref, rec_in_ref, short_ref, rec_ref, pull_ref, grad_ref, rounded_ref
):
    def load(j, carry):
        at = pl.ds(pl.multiple_of(j * 256, 256), 256)
        rec = rec_in_ref[at, :]
        rec_ref[at, :] = rec
        rounded_ref[at, :] = rec.astype(jnp.bfloat16)
        return carry

    lax.fori_loop(0, 8, load, 0)
    recourse_steps(place_ref[0], mine_ref, other_ref, rec_ref, short_ref, grad_ref, rounded_ref)

    def put(z, row):
        for q in range(Y):
            pull_ref[q, z : z + 1, :] = row

    pull_sums(aux_ref[0:1, :], rec_ref, short_ref, put)


def second_kernel(
    place_ref,
    aux_ref,
    mine_ref,
    other_ref,
    packed_ref,
    rec_in_ref,
    short_in_ref,
    pulled_ref,
    mult_ref,
    send_ref,
    rec_ref,
    pull_ref,
    short_ref,
    grad_ref,
    rounded_ref,
):
    pull_ref[0] = pulled_ref[0] + pulled_ref[1] + pulled_ref[2] + pulled_ref[3]
    eye = lanes_of((ROWS, 128)) == rows_of((ROWS, 128))
    site = rows_of((ROWS, 128)).astype(f32)

    def load(b, carry):
        at = pl.ds(pl.multiple_of(b * ROWS, ROWS), ROWS)
        index = packed_ref[b, ROWS + 8 : ROWS + 16, :]
        pull = pick(pull_ref[0, pl.ds(b // Y, 1), :], index.astype(jnp.int32) + b % Y * ROWS)
        stock = jnp.maximum(packed_ref[b, ROWS : ROWS + 8, :] + learn_rate * pull, 0.0)
        change = jnp.where(eye, -packed_ref[b, ROWS + 16 : ROWS + 17, :], 0.0)
        for k in range(8):
            change = change + jnp.where(index[k : k + 1] == site, stock[k : k + 1], 0.0)
        rec = rec_in_ref[at, :]
        rec_ref[at, :] = rec
        rounded_ref[at, :] = rec.astype(jnp.bfloat16)
        short_ref[at, :] = short_in_ref[at, :] - jnp.sum(change, axis=1, keepdims=True)
        return carry

    lax.fori_loop(0, Z * Y, load, 0, unroll=8)
    recourse_steps(place_ref[0], mine_ref, other_ref, rec_ref, short_ref, grad_ref, rounded_ref)

    def put(z, row):
        pull_ref[1, z : z + 1, :] = row

    pull_sums(aux_ref[0:1, :], rec_ref, short_ref, put)
    z = place_ref[1]
    sub = rows_of((8, 128))
    pulls = jnp.where(
        sub == 0,
        pull_ref[0, pl.ds(z, 1), :],
        jnp.where(sub == 1, pull_ref[1, pl.ds(z, 1), :], aux_ref[8:9, :]),
    )
    low = lanes_of((16, 128)) < SCEN
    for q in range(Y):
        start = pl.multiple_of((z * Y + q) * ROWS, ROWS)
        upper = rec_ref[pl.ds(start, 16), :]
        lower = rec_ref[pl.ds(start + 16, 16), :]
        pair = jnp.where(low, upper, pltpu.roll(lower, SCEN, 1))
        for g in range(GROUPS):
            send_ref[g * Y + q, 0:8, :] = mult_ref[...]
            send_ref[g * Y + q, 8:16, :] = pulls
            send_ref[g * Y + q, 16:32, :] = pair


def last_kernel(
    place_ref, got_ref, assign_ref, hold_ref, stock_ref, consensus_ref, mult_ref, rec_ref, all_ref
):
    z, y, column = place_ref[1], place_ref[2], place_ref[3]
    index = assign_ref[...] - z * (Y * ROWS)
    hold = hold_ref[...]
    start = stock_ref[...]
    totals = [got_ref[g * Y, 10:11, :] for g in range(GROUPS)]
    all_total = totals[0]
    for g in range(1, GROUPS):
        all_total = all_total + totals[g]
    mults = [got_ref[g * Y + y, 0:8, :] for g in range(GROUPS)]
    stocks = []
    weighted = jnp.zeros((8, 128), f32)
    for g in range(GROUPS):
        pull = pick(got_ref[g * Y, 8:9, :], index)
        stock = jnp.maximum(start - learn_rate * (hold + mults[g] - pull), 0.0)
        weighted = weighted + totals[g] * stock
        stocks.append(stock)
    consensus = weighted / all_total
    weighted = jnp.zeros((8, 128), f32)
    for g in range(GROUPS):
        row = got_ref[g * Y, 9:10, :]
        for q in range(1, Y):
            row = row + got_ref[g * Y + q, 9:10, :]
        pull = pick(row, index)
        apart = prox_weight * (stocks[g] - consensus)
        mults[g] = mults[g] + apart
        stock = jnp.maximum(stocks[g] - learn_rate * (hold + mults[g] - pull + apart), 0.0)
        weighted = weighted + totals[g] * stock
        stocks[g] = stock
    consensus = weighted / all_total
    consensus_ref[...] = consensus
    for g in range(GROUPS):
        all_ref[g] = mults[g] + prox_weight * (stocks[g] - consensus)
    mult_ref[...] = all_ref[column]

    low = lanes_of((16, 128)) < SCEN
    for m in range(2):
        tile = slice(m * 128, m * 128 + 128)
        even = got_ref[column * Y + 2 * m, 16:32, :]
        odd = got_ref[column * Y + 2 * m + 1, 16:32, :]
        rec_ref[0:16, tile] = jnp.where(low, even, pltpu.roll(odd, SCEN, 1))
        rec_ref[16:32, tile] = jnp.where(low, pltpu.roll(even, SCEN, 1), odd)


def run_kernel(kernel, outs, scratch, *args, hbm=0, vmem_mib=16, flops=0):
    vmem = pl.BlockSpec(memory_space=pltpu.VMEM)
    outs = [out if isinstance(out, jax.ShapeDtypeStruct) else jax.ShapeDtypeStruct(out, f32) for out in outs]
    return pl.pallas_call(
        kernel,
        out_shape=outs,
        in_specs=[pl.BlockSpec(memory_space=pltpu.SMEM)]
        + [pl.BlockSpec(memory_space=pl.ANY)] * hbm
        + [vmem] * (len(args) - 1 - hbm),
        out_specs=[vmem] * len(outs),
        scratch_shapes=[pltpu.VMEM(*entry) if isinstance(entry, tuple) else entry for entry in scratch],
        cost_estimate=pl.CostEstimate(flops=flops, bytes_accessed=0, transcendentals=0) if flops else None,
        compiler_params=pltpu.CompilerParams(vmem_limit_bytes=vmem_mib * 1024 * 1024),
    )(*args)


def one_block(always, work, *args):
    shapes = jax.eval_shape(work, *args)

    def never(*args):
        return jax.tree.map(lambda shape: jnp.zeros(shape.shape, shape.dtype), shapes)

    return lax.cond(always, work, never, *args)


def per_device(demand, recourse_init, transship, counts, assign, hold_cost, stock_init, mult_init):
    core = lax.axis_index("core")
    column = lax.axis_index("x") * CORE + core
    y = lax.axis_index("y")
    z = lax.axis_index("z")
    place = jnp.stack([core, z, y, column]).astype(jnp.int32)
    wide = (SITE_COUNT, 128)
    bf16 = jnp.bfloat16
    assign = assign.reshape(8, 128)
    hold_cost = hold_cost.reshape(8, 128)
    stock_init = stock_init.reshape(8, 128)
    mult_init = mult_init.reshape(8, 128)

    raw = (
        demand,
        recourse_init,
        counts.reshape(2, 128),
        assign,
        hold_cost,
        stock_init,
        mult_init,
    )
    packed, aux, block = run_kernel(
        prep_kernel,
        [(Y, ROWS + PARTS, 128), (16, 128), jax.ShapeDtypeStruct((Z, ROWS, COLS), bf16)],
        [(entry.shape, entry.dtype) for entry in raw]
        + [((ROWS, COLS), bf16), pltpu.SemaphoreType.DMA((8,))],
        place,
        transship,
        *raw,
        hbm=8,
        vmem_mib=60,
    )
    packed = lax.all_to_all(packed, "y", 0, 0, tiled=True)
    always = column * COLS >= 0

    def spread_z(block, packed):
        return lax.all_to_all(block, "z", 0, 0, tiled=True).reshape(Z * ROWS, COLS)

    def spread_xy(along_z):
        spread = jnp.broadcast_to(along_z[None], (X * Y, Z * ROWS, COLS))
        return lax.all_to_all(spread, ("x", "y"), 0, 0, tiled=True)

    def swap_cores(mine, gathered):
        other = lax.ppermute(mine, "core", [(0, 1), (1, 0)])
        return other, *run_kernel(unpack_kernel, [wide, wide], [], place, gathered, flops=2_000_000_000)

    gathered = lax.all_gather(packed, "z", axis=0, tiled=True)
    along_z = one_block(always, spread_z, block, packed)
    mine = one_block(always, spread_xy, along_z)
    other, rec, short = one_block(always, swap_cores, mine, gathered)

    rec, pull1 = run_kernel(
        first_kernel,
        [wide, (Y, Z, 128)],
        [(wide, f32), (wide, bf16)],
        place,
        aux,
        mine,
        other,
        rec,
        short,
    )
    pull1 = lax.all_to_all(pull1, "y", 0, 0, tiled=True)
    (send,) = run_kernel(
        second_kernel,
        [(GROUPS * Y, 32, 128)],
        [(wide, f32), ((2, Z, 128), f32), (wide, f32), (wide, f32), (wide, jnp.bfloat16)],
        place,
        aux,
        mine,
        other,
        gathered,
        rec,
        short,
        pull1,
        mult_init,
    )
    got = lax.all_to_all(send, ("x", "core", "y"), 0, 0, tiled=True)
    consensus, multipliers, recourse = run_kernel(
        last_kernel,
        [(8, 128), (8, 128), (ROWS, Y * SCEN)],
        [((GROUPS, 8, 128), f32)],
        place,
        got,
        assign,
        hold_cost,
        stock_init,
    )
    return (consensus.reshape(1024), multipliers.reshape(1, 1024), recourse)


def solution(mesh):
    grid = Mesh(mesh.devices.reshape(X, CORE, Z, Y), ("x", "core", "z", "y"))
    scen, dom = ("x", "core"), ("z", "y")
    in_specs = (
        P(dom, scen),
        P(dom, scen),
        P(dom, None),
        P(scen),
        P(dom),
        P(dom),
        P(dom),
        P(scen, dom),
    )
    out_specs = (P(dom), P(scen, dom), P(dom, scen))
    return jax.shard_map(
        per_device, mesh=grid, in_specs=in_specs, out_specs=out_specs, check_vma=False
    )
```

```python
import jax
import jax.numpy as jnp
from jax import lax
from jax.experimental import pallas as pl
from jax.experimental.pallas import tpu as pltpu
from jax.sharding import Mesh, PartitionSpec as P

SITE_COUNT = 2048
X, CORE, Z, Y = 4, 2, 16, 4
GROUPS = X * CORE
ROWS = 32
COLS = 256
SCEN = 64
PARTS = 24

penalty = 1.0
stride = 0.5
prox_weight = 2.0
learn_rate = 0.05
epsilon = 1e-05

f32 = jnp.float32


def lanes_of(shape):
    return lax.broadcasted_iota(jnp.int32, shape, len(shape) - 1)


def rows_of(shape):
    return lax.broadcasted_iota(jnp.int32, shape, len(shape) - 2)


def pick(row, index):
    return jnp.take_along_axis(
        jnp.broadcast_to(row, (8, 128)), index, axis=1, mode="promise_in_bounds"
    )


def prep_kernel(place_ref, transship_ref, *refs):
    inputs, (packed_ref, aux_ref, spread_ref), copies = refs[:7], refs[7:10], refs[10:17]
    block_ref, sems = refs[17], refs[18]
    at = pl.ds(pl.multiple_of(place_ref[3] * COLS, COLS), COLS)
    started = [
        pltpu.make_async_copy(source, target, sems.at[k])
        for k, (source, target) in enumerate(zip(inputs, copies))
    ]
    started.append(pltpu.make_async_copy(transship_ref.at[:, at], block_ref, sems.at[7]))
    for copy in started:
        copy.start()
    for copy in started:
        copy.wait()
    demand_ref, rec_ref, counts_ref, assign_ref, hold_ref, stock_ref, mult_ref = copies
    for n in range(Z):
        spread_ref[n] = block_ref[...]
    z, y = place_ref[1], place_ref[2]
    weights = counts_ref[...].astype(f32)
    total = jnp.sum(jnp.sum(weights, axis=1, keepdims=True), axis=0, keepdims=True)
    row = jnp.where(y >= 2, weights[1:2], weights[0:1])
    row = jnp.where(y % 2 == 1, pltpu.roll(row, SCEN, 1), row) / total
    row = jnp.where(lanes_of((1, 128)) < SCEN, row, 0.0)
    aux_ref[0:8, :] = jnp.broadcast_to(row, (8, 128))
    aux_ref[8:16, :] = jnp.broadcast_to(total, (8, 128))

    index = assign_ref[...] - (z * Y + y) * ROWS
    stock = stock_ref[...]
    site = rows_of((ROWS, 128))
    sums = jnp.zeros((ROWS, 128), f32)
    for k in range(8):
        sums = sums + jnp.where(index[k : k + 1] == site, stock[k : k + 1], 0.0)
    column = jnp.sum(sums, axis=1, keepdims=True)
    as_row = jnp.sum(jnp.where(lanes_of((ROWS, 128)) == site, column, 0.0), axis=0, keepdims=True)
    base = stock - learn_rate * (hold_ref[...] + mult_ref[...])
    low = lanes_of((ROWS, 128)) < SCEN
    for q in range(Y):
        tile = slice(q // 2 * 128, q // 2 * 128 + 128)
        rec = rec_ref[:, tile]
        short = demand_ref[:, tile].astype(f32) - column
        if q % 2 == 0:
            both = jnp.where(low, rec, pltpu.roll(short, SCEN, 1))
        else:
            both = jnp.where(low, pltpu.roll(rec, SCEN, 1), short)
        packed_ref[q, 0:ROWS, :] = both
        packed_ref[q, ROWS : ROWS + 8, :] = base
        packed_ref[q, ROWS + 8 : ROWS + 16, :] = index.astype(f32)
        packed_ref[q, ROWS + 16 : ROWS + 24, :] = jnp.broadcast_to(as_row, (8, 128))


def recourse_steps(core, mine_ref, other_ref, rec_ref, short_ref, grad_ref, rounded_ref):
    def one_step(inner, carry):
        square = jnp.zeros((ROWS, 128), f32)
        for y in range(Y):
            acc = jnp.zeros((512, 128), f32)
            for x in range(X):
                for ref, chunk in ((mine_ref, 2 * x + core), (other_ref, 2 * x + 1 - core)):
                    at = pl.ds(pl.multiple_of(chunk * COLS, COLS), COLS)
                    acc = acc + jnp.dot(
                        ref[x * Y + y], rounded_ref[at, :], preferred_element_type=f32
                    )
            for z in range(Z):
                at = pl.ds((z * Y + y) * ROWS, ROWS)
                grad = acc[z * ROWS : (z + 1) * ROWS] - penalty * (short_ref[at, :] - rec_ref[at, :])
                grad_ref[at, :] = grad
                square = square + grad * grad
        square = jnp.sum(square, axis=0, keepdims=True)
        factor = stride / jnp.sqrt(square / SITE_COUNT + epsilon)

        def renew(j, carry):
            at = pl.ds(pl.multiple_of(j * 256, 256), 256)
            rec = jnp.maximum(rec_ref[at, :] - grad_ref[at, :] * factor, 0.0)
            rec_ref[at, :] = rec
            rounded_ref[at, :] = rec.astype(jnp.bfloat16)
            return carry

        lax.fori_loop(0, 8, renew, 0)
        return carry

    lax.fori_loop(0, 2, one_step, 0)


def pull_sums(share, rec_ref, short_ref, put):
    for z in range(Z):
        at = pl.ds(z * 128, 128)
        gap = penalty * (short_ref[at, :] - rec_ref[at, :]) * share
        put(z, jnp.sum(gap.T, axis=0, keepdims=True))


def unpack_kernel(place_ref, packed_ref, rec_ref, short_ref):
    def load(b, carry):
        at = pl.ds(pl.multiple_of(b * ROWS, ROWS), ROWS)
        both = packed_ref[b, 0:ROWS, :]
        rec_ref[at, :] = both
        short_ref[at, :] = pltpu.roll(both, SCEN, 1)
        return carry

    lax.fori_loop(0, Z * Y, load, 0, unroll=8)


def first_kernel(
    place_ref, aux_ref, mine_ref, other_ref, rec_in_ref, short_ref, rec_ref, pull_ref, grad_ref, rounded_ref
):
    def load(j, carry):
        at = pl.ds(pl.multiple_of(j * 256, 256), 256)
        rec = rec_in_ref[at, :]
        rec_ref[at, :] = rec
        rounded_ref[at, :] = rec.astype(jnp.bfloat16)
        return carry

    lax.fori_loop(0, 8, load, 0)
    recourse_steps(place_ref[0], mine_ref, other_ref, rec_ref, short_ref, grad_ref, rounded_ref)

    def put(z, row):
        for q in range(Y):
            pull_ref[q, z : z + 1, :] = row

    pull_sums(aux_ref[0:1, :], rec_ref, short_ref, put)


def second_kernel(
    place_ref,
    aux_ref,
    mine_ref,
    other_ref,
    packed_ref,
    rec_in_ref,
    short_in_ref,
    pulled_ref,
    mult_ref,
    send_ref,
    rec_ref,
    pull_ref,
    short_ref,
    grad_ref,
    rounded_ref,
):
    pull_ref[0] = pulled_ref[0] + pulled_ref[1] + pulled_ref[2] + pulled_ref[3]
    eye = lanes_of((ROWS, 128)) == rows_of((ROWS, 128))
    site = rows_of((ROWS, 128)).astype(f32)

    def load(b, carry):
        at = pl.ds(pl.multiple_of(b * ROWS, ROWS), ROWS)
        index = packed_ref[b, ROWS + 8 : ROWS + 16, :]
        pull = pick(pull_ref[0, pl.ds(b // Y, 1), :], index.astype(jnp.int32) + b % Y * ROWS)
        stock = jnp.maximum(packed_ref[b, ROWS : ROWS + 8, :] + learn_rate * pull, 0.0)
        change = jnp.where(eye, -packed_ref[b, ROWS + 16 : ROWS + 17, :], 0.0)
        for k in range(8):
            change = change + jnp.where(index[k : k + 1] == site, stock[k : k + 1], 0.0)
        rec = rec_in_ref[at, :]
        rec_ref[at, :] = rec
        rounded_ref[at, :] = rec.astype(jnp.bfloat16)
        short_ref[at, :] = short_in_ref[at, :] - jnp.sum(change, axis=1, keepdims=True)
        return carry

    lax.fori_loop(0, Z * Y, load, 0, unroll=8)
    recourse_steps(place_ref[0], mine_ref, other_ref, rec_ref, short_ref, grad_ref, rounded_ref)

    def put(z, row):
        pull_ref[1, z : z + 1, :] = row

    pull_sums(aux_ref[0:1, :], rec_ref, short_ref, put)
    z = place_ref[1]
    sub = rows_of((8, 128))
    pulls = jnp.where(
        sub == 0,
        pull_ref[0, pl.ds(z, 1), :],
        jnp.where(sub == 1, pull_ref[1, pl.ds(z, 1), :], aux_ref[8:9, :]),
    )
    low = lanes_of((16, 128)) < SCEN
    for q in range(Y):
        start = pl.multiple_of((z * Y + q) * ROWS, ROWS)
        upper = rec_ref[pl.ds(start, 16), :]
        lower = rec_ref[pl.ds(start + 16, 16), :]
        pair = jnp.where(low, upper, pltpu.roll(lower, SCEN, 1))
        for g in range(GROUPS):
            send_ref[g * Y + q, 0:8, :] = mult_ref[...]
            send_ref[g * Y + q, 8:16, :] = pulls
            send_ref[g * Y + q, 16:32, :] = pair


def last_kernel(
    place_ref, got_ref, assign_ref, hold_ref, stock_ref, consensus_ref, mult_ref, rec_ref, all_ref
):
    z, y, column = place_ref[1], place_ref[2], place_ref[3]
    index = assign_ref[...] - z * (Y * ROWS)
    hold = hold_ref[...]
    start = stock_ref[...]
    totals = [got_ref[g * Y, 10:11, :] for g in range(GROUPS)]
    all_total = totals[0]
    for g in range(1, GROUPS):
        all_total = all_total + totals[g]
    mults = [got_ref[g * Y + y, 0:8, :] for g in range(GROUPS)]
    stocks = []
    weighted = jnp.zeros((8, 128), f32)
    for g in range(GROUPS):
        pull = pick(got_ref[g * Y, 8:9, :], index)
        stock = jnp.maximum(start - learn_rate * (hold + mults[g] - pull), 0.0)
        weighted = weighted + totals[g] * stock
        stocks.append(stock)
    consensus = weighted / all_total
    weighted = jnp.zeros((8, 128), f32)
    for g in range(GROUPS):
        row = got_ref[g * Y, 9:10, :]
        for q in range(1, Y):
            row = row + got_ref[g * Y + q, 9:10, :]
        pull = pick(row, index)
        apart = prox_weight * (stocks[g] - consensus)
        mults[g] = mults[g] + apart
        stock = jnp.maximum(stocks[g] - learn_rate * (hold + mults[g] - pull + apart), 0.0)
        weighted = weighted + totals[g] * stock
        stocks[g] = stock
    consensus = weighted / all_total
    consensus_ref[...] = consensus
    for g in range(GROUPS):
        all_ref[g] = mults[g] + prox_weight * (stocks[g] - consensus)
    mult_ref[...] = all_ref[column]

    low = lanes_of((16, 128)) < SCEN
    for m in range(2):
        tile = slice(m * 128, m * 128 + 128)
        even = got_ref[column * Y + 2 * m, 16:32, :]
        odd = got_ref[column * Y + 2 * m + 1, 16:32, :]
        rec_ref[0:16, tile] = jnp.where(low, even, pltpu.roll(odd, SCEN, 1))
        rec_ref[16:32, tile] = jnp.where(low, pltpu.roll(even, SCEN, 1), odd)


def run_kernel(kernel, outs, scratch, *args, hbm=0, vmem_mib=16, flops=0):
    vmem = pl.BlockSpec(memory_space=pltpu.VMEM)
    outs = [out if isinstance(out, jax.ShapeDtypeStruct) else jax.ShapeDtypeStruct(out, f32) for out in outs]
    return pl.pallas_call(
        kernel,
        out_shape=outs,
        in_specs=[pl.BlockSpec(memory_space=pltpu.SMEM)]
        + [pl.BlockSpec(memory_space=pl.ANY)] * hbm
        + [vmem] * (len(args) - 1 - hbm),
        out_specs=[vmem] * len(outs),
        scratch_shapes=[pltpu.VMEM(*entry) if isinstance(entry, tuple) else entry for entry in scratch],
        cost_estimate=pl.CostEstimate(flops=flops, bytes_accessed=0, transcendentals=0) if flops else None,
        compiler_params=pltpu.CompilerParams(vmem_limit_bytes=vmem_mib * 1024 * 1024),
    )(*args)


def one_block(always, work, *args):
    shapes = jax.eval_shape(work, *args)

    def never(*args):
        return jax.tree.map(lambda shape: jnp.zeros(shape.shape, shape.dtype), shapes)

    return lax.cond(always, work, never, *args)


def per_device(demand, recourse_init, transship, counts, assign, hold_cost, stock_init, mult_init):
    core = lax.axis_index("core")
    column = lax.axis_index("x") * CORE + core
    y = lax.axis_index("y")
    z = lax.axis_index("z")
    place = jnp.stack([core, z, y, column]).astype(jnp.int32)
    wide = (SITE_COUNT, 128)
    bf16 = jnp.bfloat16
    assign = assign.reshape(8, 128)
    hold_cost = hold_cost.reshape(8, 128)
    stock_init = stock_init.reshape(8, 128)
    mult_init = mult_init.reshape(8, 128)

    raw = (
        demand,
        recourse_init,
        counts.reshape(2, 128),
        assign,
        hold_cost,
        stock_init,
        mult_init,
    )
    packed, aux, block = run_kernel(
        prep_kernel,
        [(Y, ROWS + PARTS, 128), (16, 128), jax.ShapeDtypeStruct((Z, ROWS, COLS), bf16)],
        [(entry.shape, entry.dtype) for entry in raw]
        + [((ROWS, COLS), bf16), pltpu.SemaphoreType.DMA((8,))],
        place,
        transship,
        *raw,
        hbm=8,
        vmem_mib=60,
    )
    packed = lax.all_to_all(packed, "y", 0, 0, tiled=True)
    always = column * COLS >= 0

    def spread_z(block, packed):
        return lax.all_to_all(block, "z", 0, 0, tiled=True).reshape(Z * ROWS, COLS)

    def spread_xy(along_z):
        spread = jnp.broadcast_to(along_z[None], (X * Y, Z * ROWS, COLS))
        return lax.all_to_all(spread, ("x", "y"), 0, 0, tiled=True)

    def finish(mine, gathered, aux):
        other = lax.ppermute(mine, "core", [(0, 1), (1, 0)])
        rec, short = run_kernel(unpack_kernel, [wide, wide], [], place, gathered, flops=2_000_000_000)
        rec, pull1 = run_kernel(
            first_kernel,
            [wide, (Y, Z, 128)],
            [(wide, f32), (wide, bf16)],
            place,
            aux,
            mine,
            other,
            rec,
            short,
        )
        pull1 = lax.all_to_all(pull1, "y", 0, 0, tiled=True)
        (send,) = run_kernel(
            second_kernel,
            [(GROUPS * Y, 32, 128)],
            [(wide, f32), ((2, Z, 128), f32), (wide, f32), (wide, f32), (wide, jnp.bfloat16)],
            place,
            aux,
            mine,
            other,
            gathered,
            rec,
            short,
            pull1,
            mult_init,
        )
        got = lax.all_to_all(send, ("x", "core", "y"), 0, 0, tiled=True)
        consensus, multipliers, recourse = run_kernel(
            last_kernel,
            [(8, 128), (8, 128), (ROWS, Y * SCEN)],
            [((GROUPS, 8, 128), f32)],
            place,
            got,
            assign,
            hold_cost,
            stock_init,
        )
        return consensus, multipliers, recourse

    gathered = lax.all_gather(packed, "z", axis=0, tiled=True)
    along_z = one_block(always, spread_z, block, packed)
    mine = one_block(always, spread_xy, along_z)
    consensus, multipliers, recourse = one_block(always, finish, mine, gathered, aux)
    return (consensus.reshape(1024), multipliers.reshape(1, 1024), recourse)


def solution(mesh):
    grid = Mesh(mesh.devices.reshape(X, CORE, Z, Y), ("x", "core", "z", "y"))
    scen, dom = ("x", "core"), ("z", "y")
    in_specs = (
        P(dom, scen),
        P(dom, scen),
        P(dom, None),
        P(scen),
        P(dom),
        P(dom),
        P(dom),
        P(scen, dom),
    )
    out_specs = (P(dom), P(scen, dom), P(dom, scen))
    return jax.shard_map(
        per_device, mesh=grid, in_specs=in_specs, out_specs=out_specs, check_vma=False
    )
```

```python
import jax
import jax.numpy as jnp
from jax import lax
from jax.experimental import pallas as pl
from jax.experimental.pallas import tpu as pltpu
from jax.sharding import Mesh, PartitionSpec as P

SITE_COUNT = 2048
X, CORE, Z, Y = 4, 2, 16, 4
GROUPS = X * CORE
ROWS = 32
COLS = 256
SCEN = 64
PARTS = 24

penalty = 1.0
stride = 0.5
prox_weight = 2.0
learn_rate = 0.05
epsilon = 1e-05

f32 = jnp.float32


def lanes_of(shape):
    return lax.broadcasted_iota(jnp.int32, shape, len(shape) - 1)


def rows_of(shape):
    return lax.broadcasted_iota(jnp.int32, shape, len(shape) - 2)


def pick(row, index):
    return jnp.take_along_axis(
        jnp.broadcast_to(row, (8, 128)), index, axis=1, mode="promise_in_bounds"
    )


def prep_kernel(place_ref, transship_ref, *refs):
    inputs, (packed_ref, aux_ref, spread_ref), copies = refs[:7], refs[7:10], refs[10:17]
    block_ref, sems = refs[17], refs[18]
    at = pl.ds(pl.multiple_of(place_ref[3] * COLS, COLS), COLS)
    started = [
        pltpu.make_async_copy(source, target, sems.at[k])
        for k, (source, target) in enumerate(zip(inputs, copies))
    ]
    started.append(pltpu.make_async_copy(transship_ref.at[:, at], block_ref, sems.at[7]))
    for copy in started:
        copy.start()
    for copy in started:
        copy.wait()
    demand_ref, rec_ref, counts_ref, assign_ref, hold_ref, stock_ref, mult_ref = copies
    for n in range(Z):
        spread_ref[n] = block_ref[...]
    z, y = place_ref[1], place_ref[2]
    weights = counts_ref[...].astype(f32)
    total = jnp.sum(jnp.sum(weights, axis=1, keepdims=True), axis=0, keepdims=True)
    row = jnp.where(y >= 2, weights[1:2], weights[0:1])
    row = jnp.where(y % 2 == 1, pltpu.roll(row, SCEN, 1), row) / total
    row = jnp.where(lanes_of((1, 128)) < SCEN, row, 0.0)
    aux_ref[0:8, :] = jnp.broadcast_to(row, (8, 128))
    aux_ref[8:16, :] = jnp.broadcast_to(total, (8, 128))

    index = assign_ref[...] - (z * Y + y) * ROWS
    stock = stock_ref[...]
    site = rows_of((ROWS, 128))
    sums = jnp.zeros((ROWS, 128), f32)
    for k in range(8):
        sums = sums + jnp.where(index[k : k + 1] == site, stock[k : k + 1], 0.0)
    column = jnp.sum(sums, axis=1, keepdims=True)
    as_row = jnp.sum(jnp.where(lanes_of((ROWS, 128)) == site, column, 0.0), axis=0, keepdims=True)
    base = stock - learn_rate * (hold_ref[...] + mult_ref[...])
    low = lanes_of((ROWS, 128)) < SCEN
    for q in range(Y):
        tile = slice(q // 2 * 128, q // 2 * 128 + 128)
        rec = rec_ref[:, tile]
        short = demand_ref[:, tile].astype(f32) - column
        if q % 2 == 0:
            both = jnp.where(low, rec, pltpu.roll(short, SCEN, 1))
        else:
            both = jnp.where(low, pltpu.roll(rec, SCEN, 1), short)
        packed_ref[q, 0:ROWS, :] = both
        packed_ref[q, ROWS : ROWS + 8, :] = base
        packed_ref[q, ROWS + 8 : ROWS + 16, :] = index.astype(f32)
        packed_ref[q, ROWS + 16 : ROWS + 24, :] = jnp.broadcast_to(as_row, (8, 128))


def recourse_steps(core, mine_ref, other_ref, rec_ref, short_ref, grad_ref, rounded_ref):
    def one_step(inner, carry):
        square = jnp.zeros((ROWS, 128), f32)
        for y in range(Y):
            acc = jnp.zeros((512, 128), f32)
            for x in range(X):
                for ref, chunk in ((mine_ref, 2 * x + core), (other_ref, 2 * x + 1 - core)):
                    at = pl.ds(pl.multiple_of(chunk * COLS, COLS), COLS)
                    acc = acc + jnp.dot(
                        ref[x * Y + y], rounded_ref[at, :], preferred_element_type=f32
                    )
            for z in range(Z):
                at = pl.ds((z * Y + y) * ROWS, ROWS)
                grad = acc[z * ROWS : (z + 1) * ROWS] - penalty * (short_ref[at, :] - rec_ref[at, :])
                grad_ref[at, :] = grad
                square = square + grad * grad
        square = jnp.sum(square, axis=0, keepdims=True)
        factor = stride / jnp.sqrt(square / SITE_COUNT + epsilon)

        def renew(j, carry):
            at = pl.ds(pl.multiple_of(j * 256, 256), 256)
            rec = jnp.maximum(rec_ref[at, :] - grad_ref[at, :] * factor, 0.0)
            rec_ref[at, :] = rec
            rounded_ref[at, :] = rec.astype(jnp.bfloat16)
            return carry

        lax.fori_loop(0, 8, renew, 0)
        return carry

    lax.fori_loop(0, 2, one_step, 0)


def pull_sums(share, rec_ref, short_ref, put):
    for z in range(Z):
        at = pl.ds(z * 128, 128)
        gap = penalty * (short_ref[at, :] - rec_ref[at, :]) * share
        put(z, jnp.sum(gap.T, axis=0, keepdims=True))


def unpack_kernel(place_ref, packed_ref, rec_ref, short_ref):
    def load(b, carry):
        at = pl.ds(pl.multiple_of(b * ROWS, ROWS), ROWS)
        both = packed_ref[b, 0:ROWS, :]
        rec_ref[at, :] = both
        short_ref[at, :] = pltpu.roll(both, SCEN, 1)
        return carry

    lax.fori_loop(0, Z * Y, load, 0, unroll=8)


def first_kernel(
    place_ref, aux_ref, mine_ref, other_ref, rec_in_ref, short_ref, rec_ref, pull_ref, grad_ref, rounded_ref
):
    def load(j, carry):
        at = pl.ds(pl.multiple_of(j * 256, 256), 256)
        rec = rec_in_ref[at, :]
        rec_ref[at, :] = rec
        rounded_ref[at, :] = rec.astype(jnp.bfloat16)
        return carry

    lax.fori_loop(0, 8, load, 0)
    recourse_steps(place_ref[0], mine_ref, other_ref, rec_ref, short_ref, grad_ref, rounded_ref)

    def put(z, row):
        for q in range(Y):
            pull_ref[q, z : z + 1, :] = row

    pull_sums(aux_ref[0:1, :], rec_ref, short_ref, put)


def second_kernel(
    place_ref,
    aux_ref,
    mine_ref,
    other_ref,
    packed_ref,
    rec_in_ref,
    short_in_ref,
    pulled_ref,
    mult_ref,
    send_ref,
    rec_ref,
    pull_ref,
    short_ref,
    grad_ref,
    rounded_ref,
):
    pull_ref[0] = pulled_ref[0] + pulled_ref[1] + pulled_ref[2] + pulled_ref[3]
    eye = lanes_of((ROWS, 128)) == rows_of((ROWS, 128))
    site = rows_of((ROWS, 128)).astype(f32)

    def load(b, carry):
        at = pl.ds(pl.multiple_of(b * ROWS, ROWS), ROWS)
        index = packed_ref[b, ROWS + 8 : ROWS + 16, :]
        pull = pick(pull_ref[0, pl.ds(b // Y, 1), :], index.astype(jnp.int32) + b % Y * ROWS)
        stock = jnp.maximum(packed_ref[b, ROWS : ROWS + 8, :] + learn_rate * pull, 0.0)
        change = jnp.where(eye, -packed_ref[b, ROWS + 16 : ROWS + 17, :], 0.0)
        for k in range(8):
            change = change + jnp.where(index[k : k + 1] == site, stock[k : k + 1], 0.0)
        rec = rec_in_ref[at, :]
        rec_ref[at, :] = rec
        rounded_ref[at, :] = rec.astype(jnp.bfloat16)
        short_ref[at, :] = short_in_ref[at, :] - jnp.sum(change, axis=1, keepdims=True)
        return carry

    lax.fori_loop(0, Z * Y, load, 0, unroll=8)
    recourse_steps(place_ref[0], mine_ref, other_ref, rec_ref, short_ref, grad_ref, rounded_ref)

    def put(z, row):
        pull_ref[1, z : z + 1, :] = row

    pull_sums(aux_ref[0:1, :], rec_ref, short_ref, put)
    z, column = place_ref[1], place_ref[3]
    mult = jnp.concatenate([mult_ref[...], mult_ref[...]], axis=0)
    sub = rows_of((8, 128))
    pulls = jnp.where(
        sub == 0,
        pull_ref[0, pl.ds(z, 1), :],
        jnp.where(sub == 1, pull_ref[1, pl.ds(z, 1), :], aux_ref[8:9, :]),
    )
    low = lanes_of((16, 128)) < SCEN
    for q in range(Y):
        start = pl.multiple_of((z * Y + q) * ROWS, ROWS)
        upper = rec_ref[pl.ds(start, 16), :]
        lower = rec_ref[pl.ds(start + 16, 16), :]
        pair = jnp.where(low, upper, pltpu.roll(lower, SCEN, 1))
        for g in range(GROUPS):
            send_ref[g * Y + q, 0:16, :] = jnp.where(column == g, pair, mult)
            send_ref[g * Y + q, 16:24, :] = pulls


def last_kernel(
    place_ref, got_ref, assign_ref, hold_ref, stock_ref, own_ref, consensus_ref, mult_ref, rec_ref, all_ref
):
    z, y, column = place_ref[1], place_ref[2], place_ref[3]
    index = assign_ref[...] - z * (Y * ROWS)
    hold = hold_ref[...]
    start = stock_ref[...]
    totals = [got_ref[g * Y, 18:19, :] for g in range(GROUPS)]
    all_total = totals[0]
    for g in range(1, GROUPS):
        all_total = all_total + totals[g]
    mults = [
        jnp.where(column == g, own_ref[...], got_ref[g * Y + y, 0:8, :]) for g in range(GROUPS)
    ]
    stocks = []
    weighted = jnp.zeros((8, 128), f32)
    for g in range(GROUPS):
        pull = pick(got_ref[g * Y, 16:17, :], index)
        stock = jnp.maximum(start - learn_rate * (hold + mults[g] - pull), 0.0)
        weighted = weighted + totals[g] * stock
        stocks.append(stock)
    consensus = weighted / all_total
    weighted = jnp.zeros((8, 128), f32)
    for g in range(GROUPS):
        row = got_ref[g * Y, 17:18, :]
        for q in range(1, Y):
            row = row + got_ref[g * Y + q, 17:18, :]
        pull = pick(row, index)
        apart = prox_weight * (stocks[g] - consensus)
        mults[g] = mults[g] + apart
        stock = jnp.maximum(stocks[g] - learn_rate * (hold + mults[g] - pull + apart), 0.0)
        weighted = weighted + totals[g] * stock
        stocks[g] = stock
    consensus = weighted / all_total
    consensus_ref[...] = consensus
    for g in range(GROUPS):
        all_ref[g] = mults[g] + prox_weight * (stocks[g] - consensus)
    mult_ref[...] = all_ref[column]

    low = lanes_of((16, 128)) < SCEN
    for m in range(2):
        tile = slice(m * 128, m * 128 + 128)
        even = got_ref[column * Y + 2 * m, 0:16, :]
        odd = got_ref[column * Y + 2 * m + 1, 0:16, :]
        rec_ref[0:16, tile] = jnp.where(low, even, pltpu.roll(odd, SCEN, 1))
        rec_ref[16:32, tile] = jnp.where(low, pltpu.roll(even, SCEN, 1), odd)


def run_kernel(kernel, outs, scratch, *args, hbm=0, vmem_mib=16, flops=0):
    vmem = pl.BlockSpec(memory_space=pltpu.VMEM)
    outs = [out if isinstance(out, jax.ShapeDtypeStruct) else jax.ShapeDtypeStruct(out, f32) for out in outs]
    return pl.pallas_call(
        kernel,
        out_shape=outs,
        in_specs=[pl.BlockSpec(memory_space=pltpu.SMEM)]
        + [pl.BlockSpec(memory_space=pl.ANY)] * hbm
        + [vmem] * (len(args) - 1 - hbm),
        out_specs=[vmem] * len(outs),
        scratch_shapes=[pltpu.VMEM(*entry) if isinstance(entry, tuple) else entry for entry in scratch],
        cost_estimate=pl.CostEstimate(flops=flops, bytes_accessed=0, transcendentals=0) if flops else None,
        compiler_params=pltpu.CompilerParams(vmem_limit_bytes=vmem_mib * 1024 * 1024),
    )(*args)


def one_block(always, work, *args):
    shapes = jax.eval_shape(work, *args)

    def never(*args):
        return jax.tree.map(lambda shape: jnp.zeros(shape.shape, shape.dtype), shapes)

    return lax.cond(always, work, never, *args)


def per_device(demand, recourse_init, transship, counts, assign, hold_cost, stock_init, mult_init):
    core = lax.axis_index("core")
    column = lax.axis_index("x") * CORE + core
    y = lax.axis_index("y")
    z = lax.axis_index("z")
    place = jnp.stack([core, z, y, column]).astype(jnp.int32)
    wide = (SITE_COUNT, 128)
    bf16 = jnp.bfloat16
    assign = assign.reshape(8, 128)
    hold_cost = hold_cost.reshape(8, 128)
    stock_init = stock_init.reshape(8, 128)
    mult_init = mult_init.reshape(8, 128)

    raw = (
        demand,
        recourse_init,
        counts.reshape(2, 128),
        assign,
        hold_cost,
        stock_init,
        mult_init,
    )
    packed, aux, block = run_kernel(
        prep_kernel,
        [(Y, ROWS + PARTS, 128), (16, 128), jax.ShapeDtypeStruct((Z, ROWS, COLS), bf16)],
        [(entry.shape, entry.dtype) for entry in raw]
        + [((ROWS, COLS), bf16), pltpu.SemaphoreType.DMA((8,))],
        place,
        transship,
        *raw,
        hbm=8,
        vmem_mib=60,
    )
    packed = lax.all_to_all(packed, "y", 0, 0, tiled=True)
    always = column * COLS >= 0

    def spread_z(block, packed):
        return lax.all_to_all(block, "z", 0, 0, tiled=True).reshape(Z * ROWS, COLS)

    def spread_xy(along_z):
        spread = jnp.broadcast_to(along_z[None], (X * Y, Z * ROWS, COLS))
        return lax.all_to_all(spread, ("x", "y"), 0, 0, tiled=True)

    def finish(mine, gathered, aux):
        other = lax.ppermute(mine, "core", [(0, 1), (1, 0)])
        rec, short = run_kernel(unpack_kernel, [wide, wide], [], place, gathered, flops=2_000_000_000)
        rec, pull1 = run_kernel(
            first_kernel,
            [wide, (Y, Z, 128)],
            [(wide, f32), (wide, bf16)],
            place,
            aux,
            mine,
            other,
            rec,
            short,
        )
        pull1 = lax.all_to_all(pull1, "y", 0, 0, tiled=True)
        (send,) = run_kernel(
            second_kernel,
            [(GROUPS * Y, 24, 128)],
            [(wide, f32), ((2, Z, 128), f32), (wide, f32), (wide, f32), (wide, jnp.bfloat16)],
            place,
            aux,
            mine,
            other,
            gathered,
            rec,
            short,
            pull1,
            mult_init,
        )
        got = lax.all_to_all(send, ("x", "core", "y"), 0, 0, tiled=True)
        consensus, multipliers, recourse = run_kernel(
            last_kernel,
            [(8, 128), (8, 128), (ROWS, Y * SCEN)],
            [((GROUPS, 8, 128), f32)],
            place,
            got,
            assign,
            hold_cost,
            stock_init,
            mult_init,
        )
        return consensus, multipliers, recourse

    gathered = lax.all_gather(packed, "z", axis=0, tiled=True)
    along_z = one_block(always, spread_z, block, packed)
    mine = one_block(always, spread_xy, along_z)
    consensus, multipliers, recourse = one_block(always, finish, mine, gathered, aux)
    return (consensus.reshape(1024), multipliers.reshape(1, 1024), recourse)


def solution(mesh):
    grid = Mesh(mesh.devices.reshape(X, CORE, Z, Y), ("x", "core", "z", "y"))
    scen, dom = ("x", "core"), ("z", "y")
    in_specs = (
        P(dom, scen),
        P(dom, scen),
        P(dom, None),
        P(scen),
        P(dom),
        P(dom),
        P(dom),
        P(scen, dom),
    )
    out_specs = (P(dom), P(scen, dom), P(dom, scen))
    return jax.shard_map(
        per_device, mesh=grid, in_specs=in_specs, out_specs=out_specs, check_vma=False
    )
```

```python
import jax
import jax.numpy as jnp
from jax import lax
from jax.experimental import pallas as pl
from jax.experimental.pallas import tpu as pltpu
from jax.sharding import Mesh, PartitionSpec as P

SITE_COUNT = 2048
X, CORE, Z, Y = 4, 2, 16, 4
GROUPS = X * CORE
ROWS = 32
COLS = 256
SCEN = 64
PARTS = 24

penalty = 1.0
stride = 0.5
prox_weight = 2.0
learn_rate = 0.05
epsilon = 1e-05

f32 = jnp.float32


def lanes_of(shape):
    return lax.broadcasted_iota(jnp.int32, shape, len(shape) - 1)


def rows_of(shape):
    return lax.broadcasted_iota(jnp.int32, shape, len(shape) - 2)


def pick(row, index):
    return jnp.take_along_axis(
        jnp.broadcast_to(row, (8, 128)), index, axis=1, mode="promise_in_bounds"
    )


def prep_kernel(place_ref, transship_ref, *refs):
    inputs, (packed_ref, aux_ref, spread_ref), copies = refs[:7], refs[7:10], refs[10:17]
    block_ref, sems = refs[17], refs[18]
    at = pl.ds(pl.multiple_of(place_ref[3] * COLS, COLS), COLS)
    started = [
        pltpu.make_async_copy(source, target, sems.at[k])
        for k, (source, target) in enumerate(zip(inputs, copies))
    ]
    started.append(pltpu.make_async_copy(transship_ref.at[:, at], block_ref, sems.at[7]))
    for copy in started:
        copy.start()
    for copy in started:
        copy.wait()
    demand_ref, rec_ref, counts_ref, assign_ref, hold_ref, stock_ref, mult_ref = copies
    for n in range(Z):
        spread_ref[n] = block_ref[...]
    z, y = place_ref[1], place_ref[2]
    weights = counts_ref[...].astype(f32)
    total = jnp.sum(jnp.sum(weights, axis=1, keepdims=True), axis=0, keepdims=True)
    row = jnp.where(y >= 2, weights[1:2], weights[0:1])
    row = jnp.where(y % 2 == 1, pltpu.roll(row, SCEN, 1), row) / total
    row = jnp.where(lanes_of((1, 128)) < SCEN, row, 0.0)
    aux_ref[0:8, :] = jnp.broadcast_to(row, (8, 128))
    aux_ref[8:16, :] = jnp.broadcast_to(total, (8, 128))

    index = assign_ref[...] - (z * Y + y) * ROWS
    stock = stock_ref[...]
    site = rows_of((ROWS, 128))
    sums = jnp.zeros((ROWS, 128), f32)
    for k in range(8):
        sums = sums + jnp.where(index[k : k + 1] == site, stock[k : k + 1], 0.0)
    column = jnp.sum(sums, axis=1, keepdims=True)
    as_row = jnp.sum(jnp.where(lanes_of((ROWS, 128)) == site, column, 0.0), axis=0, keepdims=True)
    base = stock - learn_rate * (hold_ref[...] + mult_ref[...])
    low = lanes_of((ROWS, 128)) < SCEN
    for q in range(Y):
        tile = slice(q // 2 * 128, q // 2 * 128 + 128)
        rec = rec_ref[:, tile]
        short = demand_ref[:, tile].astype(f32) - column
        if q % 2 == 0:
            both = jnp.where(low, rec, pltpu.roll(short, SCEN, 1))
        else:
            both = jnp.where(low, pltpu.roll(rec, SCEN, 1), short)
        packed_ref[q, 0:ROWS, :] = both
        packed_ref[q, ROWS : ROWS + 8, :] = base
        packed_ref[q, ROWS + 8 : ROWS + 16, :] = index.astype(f32)
        packed_ref[q, ROWS + 16 : ROWS + 24, :] = jnp.broadcast_to(as_row, (8, 128))


def recourse_steps(core, mine_ref, other_ref, rec_ref, short_ref, grad_ref, rounded_ref):
    def one_step(inner, carry):
        square = jnp.zeros((ROWS, 128), f32)
        for y in range(Y):
            acc = jnp.zeros((512, 128), f32)
            for x in range(X):
                for ref, chunk in ((mine_ref, 2 * x + core), (other_ref, 2 * x + 1 - core)):
                    at = pl.ds(pl.multiple_of(chunk * COLS, COLS), COLS)
                    acc = acc + jnp.dot(
                        ref[x * Y + y], rounded_ref[at, :], preferred_element_type=f32
                    )
            for z in range(Z):
                at = pl.ds((z * Y + y) * ROWS, ROWS)
                grad = acc[z * ROWS : (z + 1) * ROWS] - penalty * (short_ref[at, :] - rec_ref[at, :])
                grad_ref[at, :] = grad
                square = square + grad * grad
        square = jnp.sum(square, axis=0, keepdims=True)
        factor = stride / jnp.sqrt(square / SITE_COUNT + epsilon)

        def renew(j, carry):
            at = pl.ds(pl.multiple_of(j * 256, 256), 256)
            rec = jnp.maximum(rec_ref[at, :] - grad_ref[at, :] * factor, 0.0)
            rec_ref[at, :] = rec
            rounded_ref[at, :] = rec.astype(jnp.bfloat16)
            return carry

        lax.fori_loop(0, 8, renew, 0)
        return carry

    lax.fori_loop(0, 2, one_step, 0)


def pull_sums(share, rec_ref, short_ref, put):
    for z in range(Z):
        at = pl.ds(z * 128, 128)
        gap = penalty * (short_ref[at, :] - rec_ref[at, :]) * share
        put(z, jnp.sum(gap.T, axis=0, keepdims=True))


def unpack_kernel(place_ref, packed_ref, rec_ref, short_ref):
    def load(b, carry):
        at = pl.ds(pl.multiple_of(b * ROWS, ROWS), ROWS)
        both = packed_ref[b, 0:ROWS, :]
        rec_ref[at, :] = both
        short_ref[at, :] = pltpu.roll(both, SCEN, 1)
        return carry

    lax.fori_loop(0, Z * Y, load, 0, unroll=8)


def first_kernel(
    place_ref, aux_ref, mine_ref, other_ref, rec_in_ref, short_ref, rec_ref, pull_ref, grad_ref, rounded_ref
):
    def load(j, carry):
        at = pl.ds(pl.multiple_of(j * 256, 256), 256)
        rec = rec_in_ref[at, :]
        rec_ref[at, :] = rec
        rounded_ref[at, :] = rec.astype(jnp.bfloat16)
        return carry

    lax.fori_loop(0, 8, load, 0)
    recourse_steps(place_ref[0], mine_ref, other_ref, rec_ref, short_ref, grad_ref, rounded_ref)

    def put(z, row):
        for q in range(Y):
            pull_ref[q, z : z + 1, :] = row

    pull_sums(aux_ref[0:1, :], rec_ref, short_ref, put)


def second_kernel(
    place_ref,
    aux_ref,
    mine_ref,
    other_ref,
    packed_ref,
    rec_in_ref,
    short_in_ref,
    pulled_ref,
    mult_ref,
    send_ref,
    own_pull_ref,
    own_short_ref,
    rec_ref,
    pull_ref,
    short_ref,
    grad_ref,
    rounded_ref,
):
    pull_ref[0] = pulled_ref[0] + pulled_ref[1] + pulled_ref[2] + pulled_ref[3]
    eye = lanes_of((ROWS, 128)) == rows_of((ROWS, 128))
    site = rows_of((ROWS, 128)).astype(f32)

    def load(b, carry):
        at = pl.ds(pl.multiple_of(b * ROWS, ROWS), ROWS)
        index = packed_ref[b, ROWS + 8 : ROWS + 16, :]
        pull = pick(pull_ref[0, pl.ds(b // Y, 1), :], index.astype(jnp.int32) + b % Y * ROWS)
        stock = jnp.maximum(packed_ref[b, ROWS : ROWS + 8, :] + learn_rate * pull, 0.0)
        change = jnp.where(eye, -packed_ref[b, ROWS + 16 : ROWS + 17, :], 0.0)
        for k in range(8):
            change = change + jnp.where(index[k : k + 1] == site, stock[k : k + 1], 0.0)
        rec = rec_in_ref[at, :]
        rec_ref[at, :] = rec
        rounded_ref[at, :] = rec.astype(jnp.bfloat16)
        short_ref[at, :] = short_in_ref[at, :] - jnp.sum(change, axis=1, keepdims=True)
        return carry

    lax.fori_loop(0, Z * Y, load, 0, unroll=8)
    recourse_steps(place_ref[0], mine_ref, other_ref, rec_ref, short_ref, grad_ref, rounded_ref)

    def put(z, row):
        pull_ref[1, z : z + 1, :] = row

    pull_sums(aux_ref[0:1, :], rec_ref, short_ref, put)
    z, y, column = place_ref[1], place_ref[2], place_ref[3]
    sub = rows_of((8, 128))
    own_pull_ref[...] = jnp.broadcast_to(pull_ref[0, pl.ds(z, 1), :], (8, 128))
    own_short_ref[...] = short_ref[pl.ds(pl.multiple_of((z * Y + y) * ROWS, ROWS), ROWS), :]
    pulls = jnp.where(
        sub == 0,
        pull_ref[0, pl.ds(z, 1), :],
        jnp.where(sub == 1, pull_ref[1, pl.ds(z, 1), :], aux_ref[8:9, :]),
    )
    others = jnp.concatenate([mult_ref[...], pulls], axis=0)
    low = lanes_of((16, 128)) < SCEN
    for q in range(Y):
        start = pl.multiple_of((z * Y + q) * ROWS, ROWS)
        upper = rec_ref[pl.ds(start, 16), :]
        lower = rec_ref[pl.ds(start + 16, 16), :]
        pair = jnp.where(low, upper, pltpu.roll(lower, SCEN, 1))
        for g in range(GROUPS):
            send_ref[g * Y + q] = jnp.where(column == g, pair, others)


def last_kernel(
    place_ref,
    got_ref,
    assign_ref,
    hold_ref,
    stock_ref,
    own_mult_ref,
    own_pull_ref,
    own_short_ref,
    demand_ref,
    counts_ref,
    consensus_ref,
    mult_ref,
    rec_ref,
    all_ref,
):
    z, y, column = place_ref[1], place_ref[2], place_ref[3]
    low = lanes_of((16, 128)) < SCEN
    for m in range(2):
        tile = slice(m * 128, m * 128 + 128)
        even = got_ref[column * Y + 2 * m]
        odd = got_ref[column * Y + 2 * m + 1]
        rec_ref[0:16, tile] = jnp.where(low, even, pltpu.roll(odd, SCEN, 1))
        rec_ref[16:32, tile] = jnp.where(low, pltpu.roll(even, SCEN, 1), odd)

    weights = counts_ref[...].astype(f32)
    own_total = jnp.sum(jnp.sum(weights, axis=1, keepdims=True), axis=0, keepdims=True)
    share = weights / own_total
    demand = demand_ref[...].astype(f32)
    part = jnp.where(y >= 2, demand[:, 128:256], demand[:, 0:128])
    part = jnp.where(y % 2 == 1, pltpu.roll(part, SCEN, 1), part)
    stock_sum = (part - own_short_ref[...])[:, 0:1]
    gap = jnp.zeros((ROWS, 128), f32)
    for m in range(2):
        tile = slice(m * 128, m * 128 + 128)
        short = demand[:, tile] - stock_sum
        gap = gap + penalty * (short - rec_ref[:, tile]) * share[m : m + 1]
    gap = jnp.sum(gap, axis=1, keepdims=True)
    own = lanes_of((ROWS, 128)) == rows_of((ROWS, 128)) + y * ROWS
    own_last = jnp.sum(jnp.where(own, gap, 0.0), axis=0, keepdims=True)

    def from_group(g, mine, theirs):
        return jnp.where(column == g, mine, theirs)

    index = assign_ref[...] - z * (Y * ROWS)
    hold = hold_ref[...]
    start = stock_ref[...]
    own_total = jnp.broadcast_to(own_total, (1, 128))
    totals = [from_group(g, own_total, got_ref[g * Y, 10:11, :]) for g in range(GROUPS)]
    all_total = totals[0]
    for g in range(1, GROUPS):
        all_total = all_total + totals[g]
    mults = [from_group(g, own_mult_ref[...], got_ref[g * Y + y, 0:8, :]) for g in range(GROUPS)]
    stocks = []
    weighted = jnp.zeros((8, 128), f32)
    for g in range(GROUPS):
        pull = pick(from_group(g, own_pull_ref[0:1, :], got_ref[g * Y, 8:9, :]), index)
        stock = jnp.maximum(start - learn_rate * (hold + mults[g] - pull), 0.0)
        weighted = weighted + totals[g] * stock
        stocks.append(stock)
    consensus = weighted / all_total
    weighted = jnp.zeros((8, 128), f32)
    for g in range(GROUPS):
        row = got_ref[g * Y, 9:10, :]
        for q in range(1, Y):
            row = row + got_ref[g * Y + q, 9:10, :]
        pull = pick(from_group(g, own_last, row), index)
        apart = prox_weight * (stocks[g] - consensus)
        mults[g] = mults[g] + apart
        stock = jnp.maximum(stocks[g] - learn_rate * (hold + mults[g] - pull + apart), 0.0)
        weighted = weighted + totals[g] * stock
        stocks[g] = stock
    consensus = weighted / all_total
    consensus_ref[...] = consensus
    for g in range(GROUPS):
        all_ref[g] = mults[g] + prox_weight * (stocks[g] - consensus)
    mult_ref[...] = all_ref[column]


def run_kernel(kernel, outs, scratch, *args, hbm=0, vmem_mib=16, flops=0):
    vmem = pl.BlockSpec(memory_space=pltpu.VMEM)
    outs = [out if isinstance(out, jax.ShapeDtypeStruct) else jax.ShapeDtypeStruct(out, f32) for out in outs]
    return pl.pallas_call(
        kernel,
        out_shape=outs,
        in_specs=[pl.BlockSpec(memory_space=pltpu.SMEM)]
        + [pl.BlockSpec(memory_space=pl.ANY)] * hbm
        + [vmem] * (len(args) - 1 - hbm),
        out_specs=[vmem] * len(outs),
        scratch_shapes=[pltpu.VMEM(*entry) if isinstance(entry, tuple) else entry for entry in scratch],
        cost_estimate=pl.CostEstimate(flops=flops, bytes_accessed=0, transcendentals=0) if flops else None,
        compiler_params=pltpu.CompilerParams(vmem_limit_bytes=vmem_mib * 1024 * 1024),
    )(*args)


def one_block(always, work, *args):
    shapes = jax.eval_shape(work, *args)

    def never(*args):
        return jax.tree.map(lambda shape: jnp.zeros(shape.shape, shape.dtype), shapes)

    return lax.cond(always, work, never, *args)


def per_device(demand, recourse_init, transship, counts, assign, hold_cost, stock_init, mult_init):
    core = lax.axis_index("core")
    column = lax.axis_index("x") * CORE + core
    y = lax.axis_index("y")
    z = lax.axis_index("z")
    place = jnp.stack([core, z, y, column]).astype(jnp.int32)
    wide = (SITE_COUNT, 128)
    bf16 = jnp.bfloat16
    assign = assign.reshape(8, 128)
    hold_cost = hold_cost.reshape(8, 128)
    stock_init = stock_init.reshape(8, 128)
    mult_init = mult_init.reshape(8, 128)

    raw = (
        demand,
        recourse_init,
        counts.reshape(2, 128),
        assign,
        hold_cost,
        stock_init,
        mult_init,
    )
    packed, aux, block = run_kernel(
        prep_kernel,
        [(Y, ROWS + PARTS, 128), (16, 128), jax.ShapeDtypeStruct((Z, ROWS, COLS), bf16)],
        [(entry.shape, entry.dtype) for entry in raw]
        + [((ROWS, COLS), bf16), pltpu.SemaphoreType.DMA((8,))],
        place,
        transship,
        *raw,
        hbm=8,
        vmem_mib=60,
    )
    packed = lax.all_to_all(packed, "y", 0, 0, tiled=True)
    always = column * COLS >= 0

    def spread_z(block, packed):
        return lax.all_to_all(block, "z", 0, 0, tiled=True).reshape(Z * ROWS, COLS)

    def spread_xy(along_z):
        spread = jnp.broadcast_to(along_z[None], (X * Y, Z * ROWS, COLS))
        return lax.all_to_all(spread, ("x", "y"), 0, 0, tiled=True)

    def finish(mine, gathered, aux):
        other = lax.ppermute(mine, "core", [(0, 1), (1, 0)])
        rec, short = run_kernel(unpack_kernel, [wide, wide], [], place, gathered, flops=2_000_000_000)
        rec, pull1 = run_kernel(
            first_kernel,
            [wide, (Y, Z, 128)],
            [(wide, f32), (wide, bf16)],
            place,
            aux,
            mine,
            other,
            rec,
            short,
        )
        pull1 = lax.all_to_all(pull1, "y", 0, 0, tiled=True)
        send, own_pull, own_short = run_kernel(
            second_kernel,
            [(GROUPS * Y, 16, 128), (8, 128), (ROWS, 128)],
            [(wide, f32), ((2, Z, 128), f32), (wide, f32), (wide, f32), (wide, jnp.bfloat16)],
            place,
            aux,
            mine,
            other,
            gathered,
            rec,
            short,
            pull1,
            mult_init,
        )
        got = lax.all_to_all(send, ("x", "core", "y"), 0, 0, tiled=True)
        consensus, multipliers, recourse = run_kernel(
            last_kernel,
            [(8, 128), (8, 128), (ROWS, Y * SCEN)],
            [((GROUPS, 8, 128), f32)],
            place,
            got,
            assign,
            hold_cost,
            stock_init,
            mult_init,
            own_pull,
            own_short,
            demand,
            counts.reshape(2, 128),
        )
        return consensus, multipliers, recourse

    gathered = lax.all_gather(packed, "z", axis=0, tiled=True)
    along_z = one_block(always, spread_z, block, packed)
    mine = one_block(always, spread_xy, along_z)
    consensus, multipliers, recourse = one_block(always, finish, mine, gathered, aux)
    return (consensus.reshape(1024), multipliers.reshape(1, 1024), recourse)


def solution(mesh):
    grid = Mesh(mesh.devices.reshape(X, CORE, Z, Y), ("x", "core", "z", "y"))
    scen, dom = ("x", "core"), ("z", "y")
    in_specs = (
        P(dom, scen),
        P(dom, scen),
        P(dom, None),
        P(scen),
        P(dom),
        P(dom),
        P(dom),
        P(scen, dom),
    )
    out_specs = (P(dom), P(scen, dom), P(dom, scen))
    return jax.shard_map(
        per_device, mesh=grid, in_specs=in_specs, out_specs=out_specs, check_vma=False
    )
```
